32 devices in a mesh: tp: 16 (over z, y, core), ep: 2 (over x).
Axes of the slice: x: 2, y: 2, z: 4, core: 2. Of those that a mesh axis runs over, the one named last changes fastest.
Arguments:
- residual: bfloat16 [2, 7168, 256], P('ep', 'tp')
- out_grad: bfloat16 [2, 7168, 256], P('ep', 'tp'), may hold values from -6 to 6
- norm_gain: float32 [7168], P('tp'), may hold values from 0.25 to 1.75
- context: bfloat16 [2, 16384, 256], P('ep', 'tp'), may hold values from -0.625 to 0.625
- w_out: bfloat16 [7168, 16384], P('ep', 'tp'), may hold values from -0.046875 to 0.046875
- w_gate: bfloat16 [2, 7168, 2048], P('ep', 'tp'), may hold values from -0.0625 to 0.0625
- w_up: bfloat16 [2, 7168, 2048], P('ep', 'tp'), may hold values from -0.0625 to 0.0625
- w_down: bfloat16 [2, 7168, 2048], P('ep', 'tp'), may hold values from -0.125 to 0.125
- slot_token: int32 [2, 2, 8], P('ep'), may hold values from 0 to 255, as said below
- slot_count: int32 [2, 2], P('ep'), may hold values from 1 to 8, as said below
- slot_gate: float32 [2, 2, 8], P('ep'), may hold values from 0.25 to 2.5
Outputs:
- resid_grad: bfloat16 [2, 7168, 256], P('ep', 'tp')
- context_grad: bfloat16 [2, 16384, 256], P('ep', 'tp')
- w_out_grad: bfloat16 [7168, 16384], P('ep', 'tp')
- gate_grad: bfloat16 [2, 7168, 2048], P('ep', 'tp')
- up_grad: bfloat16 [2, 7168, 2048], P('ep', 'tp')
- down_grad: bfloat16 [2, 7168, 2048], P('ep', 'tp')
The draws below stay inside these ranges and needn't reach their ends.
Inputs may be any that keep to these rules, and one draw needn't show every extreme that they name: `slot_token`: within one group and expert the 8 token positions are distinct; slots at or beyond slot_count are unused. `slot_count`: in every draw one expert has 8 tokens from every group.
All inputs are finite; a program needn't handle non-finite values.
Results may differ from the reference program's by a relative error of at most 0.014.
Values may be sent and summed in bfloat16 or wider, within the bound.
No kernel may reach another device: no remote copies, remote signals or barrier semaphores. Data moves between devices by JAX's collectives and lax.ppermute only.
A program may use at most 128 MiB of HBM per device.

```python
import math
import jax
import jax.numpy as jnp
from jax import lax

D = 7168
EXP_HIDDEN = 2048
GROUP = 256
CAP = 8
ATT = 16384
GROUPS = 2
EXPERTS = 2


def draw_residual(key, part):
    feature_idx = jnp.arange(D, dtype=jnp.float32) / max(D - 1, 1)
    rising = 20.0 ** feature_idx
    noise = jnp.clip(jax.random.normal(jax.random.fold_in(key, 31), (GROUPS, D, GROUP), jnp.float32), -4.0, 4.0)
    token_scale = jnp.exp(jax.random.uniform(jax.random.fold_in(key, 32), (GROUPS, 1, GROUP), jnp.float32, 0.0, 1.6))
    return (0.3 * noise * rising[None, :, None] * token_scale).astype(jnp.bfloat16)


def draw_slot_token(key, part):
    subkeys = jax.random.split(jax.random.fold_in(key, 11), GROUPS * EXPERTS)
    orders = jax.vmap(lambda sub: jax.random.permutation(sub, GROUP))(subkeys)
    return orders[:, :CAP].reshape(GROUPS, EXPERTS, CAP).astype(jnp.int32)


def draw_slot_count(key, part):
    baseline = jax.random.randint(jax.random.fold_in(key, 21), (GROUPS, EXPERTS), 1, CAP // 2 + 1)
    busiest = jax.random.randint(jax.random.fold_in(key, 22), (), 0, EXPERTS)
    chosen = jnp.arange(EXPERTS)[None, :] == busiest
    return jnp.where(chosen, CAP, baseline).astype(jnp.int32)


def block_levels(key, dims, cuts, least, largest):
    def one(dim, shards_of):
        draws = jax.random.uniform(jax.random.fold_in(jax.random.fold_in(key, 6), dim), (shards_of,), jnp.float32, least / len(cuts), largest / len(cuts))
        return jnp.repeat(jnp.exp(draws), dims[dim] // shards_of).reshape((-1,) + (1,) * (len(dims) - dim - 1))

    level = one(*cuts[0])
    for cut in cuts[1:]:
        level = level * one(*cut)
    return level


def bell_draw(key, extent, scale, limit, pieces=(), held_as=jnp.bfloat16):
    array = jax.random.normal(key, extent, jnp.float32) * scale
    if len(pieces) > 0:
        array = block_levels(key, extent, pieces, -0.22, 0.18) * array
    return jnp.clip(array, min=-limit, max=limit).astype(held_as)


def setup_inputs(seed: int = 0) -> dict:
    keys = jax.random.split(jax.random.key(seed), 12)
    return {
        "residual": draw_residual(jax.random.fold_in(keys[11], 71), 0),
        "out_grad": bell_draw(keys[1], (GROUPS, D, GROUP), 1.0, 6.0, ((0, 2), (1, 16))),
        "norm_gain": jnp.clip(1.0 + 0.15 * jax.random.normal(keys[2], (D,), jnp.float32), 0.25, 1.75),
        "context": bell_draw(keys[3], (GROUPS, ATT, GROUP), ((GROUPS * GROUP) ** -0.5), 0.625, ((0, 2), (1, 16))),
        "w_out": bell_draw(keys[4], (D, ATT), ATT ** -0.5, 0.046875, ((0, 2), (1, 16))),
        "w_gate": bell_draw(keys[5], (EXPERTS, D, EXP_HIDDEN), D ** -0.5, 0.0625, ((0, 2), (1, 16))),
        "w_up": bell_draw(keys[6], (EXPERTS, D, EXP_HIDDEN), D ** -0.5, 0.0625, ((0, 2), (1, 16))),
        "w_down": bell_draw(keys[7], (EXPERTS, D, EXP_HIDDEN), EXP_HIDDEN ** -0.5, 0.125, ((0, 2), (1, 16))),
        "slot_token": draw_slot_token(jax.random.fold_in(keys[11], 71), 0),
        "slot_count": draw_slot_count(jax.random.fold_in(keys[11], 71), 0),
        "slot_gate": jnp.clip(jnp.exp(math.log(2.5) - 2.3025851 * jax.random.uniform(keys[10], (GROUPS, EXPERTS, CAP), jnp.float32) ** block_levels(keys[10], (GROUPS, EXPERTS, CAP), ((0, 2),), -0.2, 0.2)), 0.25, 2.5),
    }


norm_eps = 1e-06

def expert_backward(operands):
    rows_x, rows_go, gate_w, up_w, down_w = operands
    pre_gate = jnp.dot(rows_x, gate_w, preferred_element_type=jnp.float32)
    pre_up = jnp.dot(rows_x, up_w, preferred_element_type=jnp.float32)
    hid_grad = jnp.dot(rows_go, down_w, preferred_element_type=jnp.float32)
    sigmoid_gate = jax.nn.sigmoid(pre_gate)
    silu_gate = pre_gate * sigmoid_gate
    hidden = (silu_gate * pre_up).astype(jnp.bfloat16)
    d_gate = (hid_grad * pre_up * sigmoid_gate * (1.0 + pre_gate * (1.0 - sigmoid_gate))).astype(jnp.bfloat16)
    d_up = (hid_grad * silu_gate).astype(jnp.bfloat16)
    down_grad = jnp.dot(rows_go.T, hidden, preferred_element_type=jnp.float32).astype(jnp.bfloat16)
    gate_grad = jnp.dot(rows_x.T, d_gate, preferred_element_type=jnp.float32).astype(jnp.bfloat16)
    up_grad = jnp.dot(rows_x.T, d_up, preferred_element_type=jnp.float32).astype(jnp.bfloat16)
    slot_back = (jnp.dot(d_gate, gate_w.T, preferred_element_type=jnp.float32) + jnp.dot(d_up, up_w.T, preferred_element_type=jnp.float32)).astype(jnp.bfloat16)
    return (slot_back, gate_grad, up_grad, down_grad)

def pick_rows(source, slot_table):
    return source[slot_table]

def add_rows(slot_table, values):
    summed = jnp.zeros((GROUP, D), jnp.float32)
    return summed.at[slot_table.reshape(-1)].add(values.reshape(-1, D).astype(jnp.float32))

def reference(residual, out_grad, norm_gain, context, w_out, w_gate, w_up, w_down, slot_token, slot_count, slot_gate):
    stream = residual.astype(jnp.float32).transpose(0, 2, 1)
    inv_rms = lax.rsqrt(lax.optimization_barrier(jnp.mean(stream * stream, axis=-1, keepdims=True)) + norm_eps)
    normed = stream * inv_rms
    inputs = (normed * norm_gain).astype(jnp.bfloat16)
    grad_in = out_grad.astype(jnp.float32).transpose(0, 2, 1)
    live_mask = (jnp.arange(CAP)[None, None, :] < slot_count[:, :, None])[..., None]
    slot_in = jnp.where(live_mask, jax.vmap(pick_rows)(inputs, slot_token), jnp.zeros((), jnp.bfloat16))
    slot_go = jnp.where(live_mask, slot_gate[..., None] * jax.vmap(pick_rows)(grad_in, slot_token), 0.0).astype(jnp.bfloat16)
    rows_x = slot_in.transpose(1, 0, 2, 3).reshape(EXPERTS, GROUPS * CAP, D)
    rows_go = slot_go.transpose(1, 0, 2, 3).reshape(EXPERTS, GROUPS * CAP, D)
    slot_back, gate_grad, up_grad, down_grad = lax.map(expert_backward, (rows_x, rows_go, w_gate, w_up, w_down))
    slot_back = slot_back.reshape(EXPERTS, GROUPS, CAP, D).transpose(1, 0, 2, 3)
    in_grad = jax.vmap(add_rows)(slot_token, slot_back).astype(jnp.bfloat16)
    scaled = in_grad.astype(jnp.float32) * norm_gain
    center = lax.optimization_barrier(jnp.mean(scaled * normed, axis=-1, keepdims=True))
    resid_tok = (grad_in + inv_rms * (scaled - normed * center)).astype(jnp.bfloat16)
    context_grad = lax.map(lambda grad_rows: jnp.dot(grad_rows, w_out, preferred_element_type=jnp.float32).astype(jnp.bfloat16).T, resid_tok)
    context_tok = context.transpose(0, 2, 1).reshape(GROUPS * GROUP, ATT)
    w_out_grad = jnp.dot(resid_tok.reshape(GROUPS * GROUP, D).T, context_tok, preferred_element_type=jnp.float32).astype(jnp.bfloat16)
    resid_grad = resid_tok.transpose(0, 2, 1)
    return (resid_grad, context_grad, w_out_grad, gate_grad, up_grad, down_grad)
```

```python
import functools

import jax
import jax.numpy as jnp
from jax import lax
from jax.experimental import pallas as pl
from jax.experimental.pallas import tpu as pltpu
from jax.sharding import PartitionSpec as P

norm_eps = 1e-06
BF = jnp.bfloat16
F32 = jnp.float32
MIB = 1024 * 1024


def mm(left, right):
    return jnp.dot(left, right, preferred_element_type=F32)


def contract_rows(left, right):
    return lax.dot_general(left, right, (((0,), (0,)), ((), ())), preferred_element_type=F32)


def contract_cols(left, right):
    return lax.dot_general(left, right, (((1,), (1,)), ((), ())), preferred_element_type=F32)


def split_two(value):
    high = value.astype(BF).astype(F32)
    rest = jnp.where(jnp.abs(value) < jnp.inf, value - high, 0.0)
    return high, rest


def lane_ids(shape):
    return lax.broadcasted_iota(jnp.int32, shape, len(shape) - 1)


def row_ids(shape):
    return lax.broadcasted_iota(jnp.int32, shape, len(shape) - 2)


def two_lanes(value, shape):
    high, rest = split_two(value)
    lane = lane_ids(shape)
    return jnp.where(lane == 0, high, jnp.where(lane == 1, rest, 0.0))


def call(kernel, outs, operands, in_specs, out_specs, grid=None, scratch=(), flops=0, limit=52):
    size = 0
    for leaf in list(outs) + list(operands):
        count = 1
        for dim in leaf.shape:
            count *= dim
        size += count * leaf.dtype.itemsize
    extra = {} if grid is None else {"grid": grid}
    return pl.pallas_call(
        kernel,
        out_shape=tuple(outs),
        in_specs=in_specs,
        out_specs=tuple(out_specs),
        scratch_shapes=list(scratch),
        compiler_params=pltpu.CompilerParams(vmem_limit_bytes=limit * MIB),
        cost_estimate=pl.CostEstimate(flops=flops, bytes_accessed=size, transcendentals=0),
        **extra,
    )(*operands)


VMEM = pl.BlockSpec(memory_space=pltpu.VMEM)
HBM = pl.BlockSpec(memory_space=pltpu.HBM)


def shape_of(shape, dtype=BF):
    return jax.ShapeDtypeStruct(shape, dtype)


def one_hot(pos, tokens):
    hit = pos.astype(jnp.int32) == lane_ids((pos.shape[0], tokens))
    return jnp.where(hit, 1.0, 0.0).astype(BF)


def pick_kernel(token_ref, count_ref, gate_ref, resid_ref, out_ref, *sends):
    experts, capacity = token_ref.shape[1:]
    feat, tokens = resid_ref.shape[1:]
    lanes = sends[0].shape[1]
    slots = experts * capacity
    ep = lax.axis_index("ep")

    def column(ref):
        rows = []
        for s in range(experts):
            e = lax.rem(ep + s, experts)
            rows.append(jnp.broadcast_to(ref[0, pl.ds(e, 1), :], (capacity, capacity)))
        rows = jnp.concatenate(rows, axis=0)
        shape = (slots, capacity)
        mine = lane_ids(shape) == lax.rem(row_ids(shape), capacity)
        return jnp.sum(jnp.where(mine, rows.astype(F32), 0.0), axis=1, keepdims=True)

    counts = jnp.sum(
        jnp.where(
            lane_ids((slots, experts))
            == lax.rem(ep + row_ids((slots, experts)) // capacity, experts),
            jnp.broadcast_to(count_ref[...], (slots, experts)),
            0,
        ).astype(F32),
        axis=1,
        keepdims=True,
    )
    order = lax.rem(row_ids((slots, 1)), capacity).astype(F32)
    pos = jnp.where(order < counts, column(token_ref), -1.0)
    hot = one_hot(pos, tokens)
    picked = contract_cols(hot, resid_ref[0])
    grads = column(gate_ref) * contract_cols(hot, out_ref[0])
    for s in range(experts):
        rows = slice(s * capacity, (s + 1) * capacity)
        sends[s][:, :feat] = jnp.concatenate([picked[rows], grads[rows]], axis=0).astype(BF)
        tail = jnp.concatenate([pos[rows], pos[rows]], axis=0)
        sends[s][:, feat:] = jnp.broadcast_to(tail, (2 * capacity, lanes - feat)).astype(BF)


def rows_of(blocks, feat):
    blocks = [b[...].astype(F32) for b in blocks]
    capacity = blocks[0].shape[0] // 2
    x = jnp.concatenate([b[:capacity, :feat] for b in blocks], axis=0)
    go = jnp.concatenate([b[capacity:, :feat] for b in blocks], axis=0)
    pos = jnp.concatenate([b[:capacity, feat : feat + 1] for b in blocks], axis=0)
    return x, go, pos


def fetch(sources, buffer, sems, steps):
    tile = buffer.shape[2] // steps
    copies = []
    for i in range(steps):
        part = slice(i * tile, (i + 1) * tile)
        row = []
        for n, source in enumerate(sources):
            row.append(
                pltpu.make_async_copy(
                    source.at[0, :, part], buffer.at[n, :, part], sems.at[n, i]
                )
            )
            row[-1].start()
        copies.append(row)
    return copies


def parts_kernel(features, groups, steps, *refs):
    got = refs[:groups]
    gain_ref, gate_ref, up_ref, down_ref, sums_ref, buffer, sems = refs[groups:]
    copies = fetch((gate_ref, up_ref, down_ref), buffer, sems, steps)
    feat = buffer.shape[1]
    low, high, _, lanes = sums_ref.shape
    count = low * high
    unit = buffer.shape[2] // count
    chunk = count // steps
    tile = unit * chunk
    x, go, _ = rows_of(got, feat)
    gained = (x * gain_ref[:1]).astype(BF)
    go = go.astype(BF)
    square = jnp.sum(x * x, axis=1, keepdims=True) / features
    tail = two_lanes(square, (x.shape[0], lanes - 3 * unit)).astype(BF)
    for i in range(steps):
        for n, rows in enumerate((gained, gained, go)):
            copies[i][n].wait()
            part = mm(rows, buffer[n, :, i * tile : (i + 1) * tile]).astype(BF)
            for k in range(chunk):
                u = i * chunk + k
                place = slice(n * unit, (n + 1) * unit)
                sums_ref[u % low, u // low, :, place] = part[:, k * unit : (k + 1) * unit]
        for k in range(chunk):
            u = i * chunk + k
            sums_ref[u % low, u // low, :, 3 * unit :] = tail


def add_kernel(parts_ref, total_ref):
    total = parts_ref[0].astype(F32)
    for k in range(1, parts_ref.shape[0]):
        total = total + parts_ref[k].astype(F32)
    total_ref[...] = total.astype(BF)


def activate(sums, unit):
    square = sums[:, 3 * unit : 3 * unit + 1] + sums[:, 3 * unit + 1 : 3 * unit + 2]
    inv_rms = lax.rsqrt(square + norm_eps)
    pre_gate = jnp.where(inv_rms > 0, sums[:, :unit] * inv_rms, 0.0)
    pre_up = jnp.where(inv_rms > 0, sums[:, unit : 2 * unit] * inv_rms, 0.0)
    hid_grad = sums[:, 2 * unit : 3 * unit]
    sigmoid_gate = 1.0 / (1.0 + jnp.exp(-pre_gate))
    silu_gate = pre_gate * sigmoid_gate
    hidden = (silu_gate * pre_up).astype(BF)
    d_gate = (hid_grad * pre_up * sigmoid_gate * (1.0 + pre_gate * (1.0 - sigmoid_gate))).astype(BF)
    d_up = (hid_grad * silu_gate).astype(BF)
    dots = jnp.sum(
        d_gate.astype(F32) * pre_gate + d_up.astype(F32) * pre_up, axis=1, keepdims=True
    )
    tail = two_lanes(dots, (sums.shape[0], sums.shape[1] - 3 * unit)).astype(BF)
    return inv_rms, jnp.concatenate([hidden, d_gate, d_up, tail], axis=1)


def act_kernel(unit, sums_ref, inv_ref, acts_ref):
    total = sums_ref[0].astype(F32)
    for k in range(1, sums_ref.shape[0]):
        total = total + sums_ref[k].astype(F32)
    inv_rms, acts = activate(total, unit)
    inv_ref[...] = jnp.broadcast_to(inv_rms, inv_ref.shape)
    for k in range(acts_ref.shape[0]):
        acts_ref[k] = acts


def delta_kernel(features, unit, groups, steps, *refs):
    got = refs[:groups]
    acts_ref, gain_ref, inv_ref, gate_ref, up_ref = refs[groups : groups + 5]
    hidden_ref, dgate_ref, dup_ref, slot_ref, go_ref, delta_ref = refs[groups + 5 : groups + 11]
    backs = refs[groups + 11 : 2 * groups + 11]
    buffer, sems = refs[2 * groups + 11 :]
    copies = fetch((gate_ref, up_ref), buffer, sems, steps)
    feat = buffer.shape[1]
    low, high = acts_ref.shape[:2]
    count = low * high
    chunk = count // steps
    tile = unit * chunk
    x, go, pos = rows_of(got, feat)
    inv_rms = inv_ref[:, :1]
    normed = x * inv_rms
    slot_ref[...] = (normed * gain_ref[:1]).astype(BF)
    go_ref[...] = go.astype(BF)
    dots = acts_ref[0, 0, :, 3 * unit : 3 * unit + 128].astype(F32)
    for u in range(1, count):
        dots = dots + acts_ref[u % low, u // low, :, 3 * unit : 3 * unit + 128].astype(F32)
    dots = (dots[:, :1] + dots[:, 1:2]) / features
    total = jnp.zeros((x.shape[0], feat), F32)
    for i in range(steps):
        part = slice(i * tile, (i + 1) * tile)
        for n, ref in enumerate((hidden_ref, dgate_ref, dup_ref)):
            place = slice(n * unit, (n + 1) * unit)
            value = jnp.concatenate(
                [acts_ref[u % low, u // low, :, place] for u in range(i * chunk, (i + 1) * chunk)],
                axis=1,
            )
            ref[:, part] = value
            if n > 0:
                copies[i][n - 1].wait()
                total = total + contract_cols(value, buffer[n - 1, :, part])
    change = inv_rms * (total * gain_ref[:1] - normed * dots)
    tail = jnp.broadcast_to(pos, (pos.shape[0], delta_ref.shape[1] - feat))
    delta_ref[:, :feat] = change.astype(BF)
    delta_ref[:, feat:] = tail.astype(BF)
    capacity = backs[0].shape[0]
    for s in range(groups):
        rows = slice(s * capacity, (s + 1) * capacity)
        backs[s][:, :feat] = change[rows]
        backs[s][:, feat:] = tail[rows]


def grads_kernel(slot_ref, go_ref, hidden_ref, dgate_ref, dup_ref, gate_out, up_out, down_out):
    gate_out[0] = contract_rows(slot_ref[...], dgate_ref[...]).astype(BF)
    up_out[0] = contract_rows(slot_ref[...], dup_ref[...]).astype(BF)
    down_out[0] = contract_rows(go_ref[...], hidden_ref[...]).astype(BF)


def back_rows(backs, feat):
    rows = jnp.concatenate([b[...] for b in backs], axis=0)
    return rows[:, :feat].astype(BF), rows[:, feat : feat + 1]


def resid_kernel(*refs):
    out_ref, resid_ref = refs[-2:]
    feat, tokens = out_ref.shape[1:]
    change, pos = back_rows(refs[:-2], feat)
    change = contract_rows(change, one_hot(pos, tokens))
    resid_ref[0] = (out_ref[0].astype(F32) + change).astype(BF)


def plain_kernel(block_ref, w_ref, *refs):
    outs, acc_ref = refs[:-1], refs[-1]
    step = pl.program_id(0)
    groups, cores, feat, tokens = block_ref.shape
    ep = lax.axis_index("ep")

    @pl.when(step == 0)
    def _():
        acc_ref[...] = jnp.zeros_like(acc_ref)

    columns = []
    for shift in range(groups):
        g = lax.rem(ep + shift, groups)
        columns.append(jnp.concatenate([block_ref[g, c] for c in range(cores)], axis=0))
    acc_ref[...] += contract_rows(jnp.concatenate(columns, axis=1), w_ref[...])

    @pl.when(step == pl.num_programs(0) - 1)
    def _():
        for shift in range(groups):
            outs[shift][...] = acc_ref[shift * tokens : (shift + 1) * tokens, :].astype(BF)


def fixed_kernel(delta_ref, w_ref, *refs):
    outs, (acc_ref, buffer, sems) = refs[:-3], refs[-3:]
    experts, quarters, cores, rows, _ = delta_ref.shape
    groups = len(outs)
    capacity = rows // groups
    height = w_ref.shape[0] // quarters
    feat = height // cores
    ep = lax.axis_index("ep")
    copies = []
    for q in range(quarters):
        part = slice(q * height, (q + 1) * height)
        copies.append(pltpu.make_async_copy(w_ref.at[part, :], buffer.at[part, :], sems.at[q]))
        copies[-1].start()
    for q in range(quarters):
        copies[q].wait()
        total = None
        for c in range(cores):
            delta = jnp.concatenate([delta_ref[e, q, c] for e in range(experts)], axis=0)
            start = q * height + c * feat
            part = mm(delta[:, :feat], buffer[start : start + feat, :])
            total = part if total is None else total + part
        acc_ref[...] = total if q == 0 else acc_ref[...] + total
    for shift in range(groups):
        pieces = []
        for s in range(experts):
            e = lax.rem(ep + shift + s, experts)
            start = pl.multiple_of(e * rows + s * capacity, 8)
            pieces.append(acc_ref[pl.ds(start, capacity), :])
        outs[shift][...] = jnp.concatenate(pieces, axis=0).astype(BF)


def weight_kernel(block_ref, delta_ref, ctx_ref, out_ref):
    groups, cores, feat, tokens = block_ref.shape
    experts, _, _, rows, _ = delta_ref.shape
    capacity = rows // groups
    ep = lax.axis_index("ep")
    columns = experts * rows
    row = row_ids((columns, 1))
    group_of = lax.rem(row // rows - lax.rem(row // capacity, groups) + groups, groups)
    for c in range(cores):
        packed = jnp.concatenate([delta_ref[e, 0, c] for e in range(experts)], axis=0)
        delta = packed[:, :feat]
        pos = packed[:, feat : feat + 1].astype(F32)
        blocks = []
        for shift in range(groups):
            g = lax.rem(ep - shift + groups, groups)
            hot = one_hot(jnp.where(group_of == g, pos, -1.0), tokens)
            change = contract_rows(delta, hot)
            blocks.append((block_ref[g, c].astype(F32) + change).astype(BF))
        total = mm(jnp.concatenate(blocks, axis=1), ctx_ref[...])
        out_ref[c * feat : (c + 1) * feat, :] = total.astype(BF)


def context_kernel(groups, *refs):
    out_ref = refs[-1]
    tokens = out_ref.shape[2]
    backs, plains, fixes = refs[:groups], refs[groups : 2 * groups], refs[2 * groups : -1]
    pos = jnp.concatenate([b[:, b.shape[1] - 1 :] for b in backs], axis=0)
    total = plains[0][...].astype(F32)
    for ref in plains[1:]:
        total = total + ref[...].astype(F32)
    hot = one_hot(pos, tokens)
    for ref in fixes:
        total = total + contract_rows(hot, ref[...])
    out_ref[0] = total.T.astype(BF)


def shards(
    residual,
    out_grad,
    norm_gain,
    context,
    w_out,
    w_gate,
    w_up,
    w_down,
    slot_token,
    slot_count,
    slot_gate,
):
    tp_count = lax.axis_size("tp")
    ep_count = lax.axis_size("ep")
    near = tp_count // ep_count
    feat, tokens = residual.shape[1:]
    features = feat * tp_count
    experts, capacity = slot_token.shape[1:]
    groups = ep_count
    slots = experts * capacity
    rows = groups * capacity
    hidden_units = w_gate.shape[2]
    unit = hidden_units // tp_count
    atts = w_out.shape[1]
    lanes = -(-(feat + 1) // 128) * 128
    gain_row = jnp.broadcast_to(norm_gain[None, :], (8, feat))
    low = 1
    while low * low < tp_count:
        low *= 2
    high = tp_count // low
    low_groups = [[a * low + b for b in range(low)] for a in range(high)]
    high_groups = [[a * low + b for a in range(high)] for b in range(low)]

    def trade(value, members):
        return lax.all_to_all(value, "tp", 0, 0, tiled=True, axis_index_groups=members)

    ahead = [[(i, (i + s) % ep_count) for i in range(ep_count)] for s in range(ep_count)]
    behind = [[(i, (i - s) % ep_count) for i in range(ep_count)] for s in range(ep_count)]

    sends = call(
        pick_kernel,
        [shape_of((2 * capacity, lanes))] * experts,
        [slot_token, slot_count, slot_gate, residual, out_grad],
        [VMEM] * 5,
        [VMEM] * experts,
        flops=4 * slots * tokens * feat,
        limit=56,
    )
    got = [sends[0]] + [lax.ppermute(sends[s], "ep", ahead[s]) for s in range(1, ep_count)]

    route = []
    for a in range(tp_count):
        for b in range(ep_count):
            route.append((a * ep_count + b, (b * near + a % near) * ep_count + a // near))
    moved = lax.ppermute(out_grad[0], ("tp", "ep"), route)

    ctx_own = context[0].T
    ctx_parts = [ctx_own] + [lax.ppermute(ctx_own, "ep", ahead[s]) for s in range(1, ep_count)]
    ctx_all = jnp.concatenate(ctx_parts, axis=0)

    steps = 4
    tile = hidden_units // steps
    wide = 3 * unit + 128
    if unit % 128 == 0:
        (sums,) = call(
            functools.partial(parts_kernel, features, groups, steps),
            [shape_of((low, high, rows, wide))],
            got + [gain_row, w_gate, w_up, w_down],
            [VMEM] * (groups + 1) + [HBM] * 3,
            [VMEM],
            scratch=[
                pltpu.VMEM((3, feat, hidden_units), BF),
                pltpu.SemaphoreType.DMA((3, steps)),
            ],
            flops=6 * rows * feat * hidden_units,
        )
    else:
        x, go, _ = rows_of(got, feat)
        gained = (x * norm_gain[None, :]).astype(BF)
        square = jnp.sum(x * x, axis=1, keepdims=True) / features
        parts = [mm(gained, w_gate[0]), mm(gained, w_up[0]), mm(go.astype(BF), w_down[0])]
        parts = [p.astype(BF).reshape(rows, tp_count, unit).transpose(1, 0, 2) for p in parts]
        tail = two_lanes(square, (rows, 128)).astype(BF)
        tail = jnp.broadcast_to(tail[None], (tp_count, rows, 128))
        sums = jnp.concatenate(parts + [tail], axis=2)
        sums = sums.reshape(high, low, rows, wide).transpose(1, 0, 2, 3)
    moved, _ = lax.optimization_barrier((moved, got[-1]))
    block = lax.all_gather(moved, "tp", axis=0).reshape(groups, near, feat, tokens)
    sums, _ = lax.optimization_barrier((sums, moved))
    (sums,) = call(add_kernel, [shape_of((high, rows, wide))], [trade(sums, low_groups)], [VMEM], [VMEM])
    sums = trade(sums, high_groups)
    if unit % 128 == 0:
        inv_rms, acts = call(
            functools.partial(act_kernel, unit),
            [shape_of((rows, 128), F32), shape_of((high, rows, wide))],
            [sums],
            [VMEM],
            [VMEM, VMEM],
        )
    else:
        inv_rms, acts = activate(jnp.sum(sums.astype(F32), axis=0), unit)
        inv_rms = jnp.broadcast_to(inv_rms, (rows, 128))
        acts = jnp.broadcast_to(acts[None], (high,) + acts.shape)
    acts = trade(acts, high_groups)
    acts = trade(jnp.broadcast_to(acts[None], (low,) + acts.shape), low_groups)
    acts, ctx_all = lax.optimization_barrier((acts, ctx_all))
    if unit % 128 == 0:
        made = call(
            functools.partial(delta_kernel, features, unit, groups, steps),
            [shape_of((rows, hidden_units))] * 3
            + [shape_of((rows, feat))] * 2
            + [shape_of((rows, lanes))]
            + [shape_of((capacity, lanes), F32)] * groups,
            got + [acts, gain_row, inv_rms, w_gate, w_up],
            [VMEM] * (groups + 3) + [HBM] * 2,
            [VMEM] * (6 + groups),
            scratch=[
                pltpu.VMEM((2, feat, hidden_units), BF),
                pltpu.SemaphoreType.DMA((2, steps)),
            ],
            flops=4 * rows * feat * hidden_units,
        )
        hidden, d_gate, d_up, slot_in, rows_go, delta = made[:6]
        backs = list(made[6:])
    else:
        x, go, pos = rows_of(got, feat)
        rows_go = go.astype(BF)
        acts = acts.transpose(1, 0, 2, 3).reshape(tp_count, rows, wide)
        hidden, d_gate, d_up = [
            acts[:, :, n * unit : (n + 1) * unit].transpose(1, 0, 2).reshape(rows, hidden_units)
            for n in range(3)
        ]
        dots = jnp.sum(acts[:, :, 3 * unit : 3 * unit + 2].astype(F32), axis=(0, 2))[:, None]
        normed = x * inv_rms[:, :1]
        slot_in = (normed * norm_gain[None, :]).astype(BF)
        slot_back = contract_cols(d_gate, w_gate[0]) + contract_cols(d_up, w_up[0])
        change = inv_rms[:, :1] * (slot_back * norm_gain[None, :] - normed * (dots / features))
        packed = jnp.concatenate([change, jnp.broadcast_to(pos, (rows, lanes - feat))], axis=1)
        delta = packed.astype(BF)
        backs = [packed[s * capacity : (s + 1) * capacity] for s in range(groups)]

    spread = lax.ppermute(delta, ("tp", "ep"), route)
    backs = [backs[0]] + [lax.ppermute(backs[s], "ep", behind[s]) for s in range(1, ep_count)]
    grads = call(
        grads_kernel,
        [shape_of((1, feat, hidden_units))] * 3,
        [slot_in, rows_go, hidden, d_gate, d_up],
        [pl.BlockSpec((rows, feat), lambda i: (0, 0))] * 2
        + [pl.BlockSpec((rows, tile), lambda i: (0, i))] * 3,
        [pl.BlockSpec((1, feat, tile), lambda i: (0, 0, i))] * 3,
        grid=(steps,),
        flops=6 * rows * feat * hidden_units,
    )
    spread, grads = lax.optimization_barrier((spread, grads))
    spread = jnp.broadcast_to(spread[None], (tp_count, rows, lanes))
    spread = lax.all_to_all(spread, "tp", split_axis=0, concat_axis=0, tiled=True)
    spread = spread.reshape(experts, near // 2, 2, rows, lanes)

    quarters = near // 2
    out_block = pl.BlockSpec((groups, 2, feat, tokens), lambda q: (0, q, 0, 0))
    delta_block = pl.BlockSpec((experts, 1, 2, rows, lanes), lambda q: (0, q, 0, 0, 0))
    w_block = pl.BlockSpec((2 * feat, atts), lambda q: (q, 0))
    plain = call(
        plain_kernel,
        [shape_of((tokens, atts))] * groups,
        [block, w_out],
        [out_block, w_block],
        [pl.BlockSpec((tokens, atts), lambda q: (0, 0))] * groups,
        grid=(quarters,),
        scratch=[pltpu.VMEM((groups * tokens, atts), F32)],
        flops=2 * groups * tokens * near * feat * atts,
        limit=52,
    )
    spread, plain = lax.optimization_barrier((spread, plain))
    plains = [plain[0]] + [lax.ppermute(plain[s], "ep", ahead[s]) for s in range(1, ep_count)]
    fixed = call(
        fixed_kernel,
        [shape_of((slots, atts))] * groups,
        [spread, w_out],
        [VMEM, HBM],
        [VMEM] * groups,
        scratch=[
            pltpu.VMEM((experts * rows, atts), F32),
            pltpu.VMEM(w_out.shape, BF),
            pltpu.SemaphoreType.DMA((quarters,)),
        ],
        flops=2 * experts * rows * near * feat * atts,
        limit=52,
    )
    spread, fixed = lax.optimization_barrier((spread, fixed))
    fixes = [fixed[0]] + [lax.ppermute(fixed[s], "ep", ahead[s]) for s in range(1, ep_count)]
    (w_out_grad,) = call(
        weight_kernel,
        [shape_of((near * feat, atts))],
        [block, spread, ctx_all],
        [out_block, delta_block, pl.BlockSpec(ctx_all.shape, lambda q: (0, 0))],
        [pl.BlockSpec((2 * feat, atts), lambda q: (q, 0))],
        grid=(quarters,),
        flops=2 * groups * tokens * near * feat * atts,
        limit=52,
    )
    (w_out_grad, backs) = lax.optimization_barrier((w_out_grad, backs))
    (resid,) = call(
        resid_kernel,
        [shape_of((1, feat, tokens))],
        backs + [out_grad],
        [VMEM] * (groups + 1),
        [VMEM],
        flops=2 * slots * feat * tokens,
    )
    (ctx_grad,) = call(
        functools.partial(context_kernel, groups),
        [shape_of((1, atts, tokens))],
        backs + plains + fixes,
        [VMEM] * (3 * groups),
        [VMEM],
        flops=2 * slots * tokens * atts,
    )
    return (resid, ctx_grad, w_out_grad) + tuple(grads)


def solution(mesh):
    return jax.shard_map(
        shards,
        mesh=mesh,
        in_specs=(
            P("ep", "tp", None),
            P("ep", "tp", None),
            P("tp"),
            P("ep", "tp", None),
            P("ep", "tp"),
            P("ep", "tp", None),
            P("ep", "tp", None),
            P("ep", "tp", None),
            P("ep", None, None),
            P("ep", None),
            P("ep", None, None),
        ),
        out_specs=(
            P("ep", "tp", None),
            P("ep", "tp", None),
            P("ep", "tp"),
            P("ep", "tp", None),
            P("ep", "tp", None),
            P("ep", "tp", None),
        ),
        check_vma=False,
    )
```

```python
import functools

import jax
import jax.numpy as jnp
from jax import lax
from jax.experimental import pallas as pl
from jax.experimental.pallas import tpu as pltpu
from jax.sharding import PartitionSpec as P

norm_eps = 1e-06
BF = jnp.bfloat16
F32 = jnp.float32
MIB = 1024 * 1024


def mm(left, right):
    return jnp.dot(left, right, preferred_element_type=F32)


def contract_rows(left, right):
    return lax.dot_general(left, right, (((0,), (0,)), ((), ())), preferred_element_type=F32)


def contract_cols(left, right):
    return lax.dot_general(left, right, (((1,), (1,)), ((), ())), preferred_element_type=F32)


def split_two(value):
    high = value.astype(BF).astype(F32)
    rest = jnp.where(jnp.abs(value) < jnp.inf, value - high, 0.0)
    return high, rest


def lane_ids(shape):
    return lax.broadcasted_iota(jnp.int32, shape, len(shape) - 1)


def row_ids(shape):
    return lax.broadcasted_iota(jnp.int32, shape, len(shape) - 2)


def two_lanes(value, shape):
    high, rest = split_two(value)
    lane = lane_ids(shape)
    return jnp.where(lane == 0, high, jnp.where(lane == 1, rest, 0.0))


def call(kernel, outs, operands, in_specs, out_specs, grid=None, scratch=(), flops=0, limit=52):
    size = 0
    for leaf in list(outs) + list(operands):
        count = 1
        for dim in leaf.shape:
            count *= dim
        size += count * leaf.dtype.itemsize
    extra = {} if grid is None else {"grid": grid}
    return pl.pallas_call(
        kernel,
        out_shape=tuple(outs),
        in_specs=in_specs,
        out_specs=tuple(out_specs),
        scratch_shapes=list(scratch),
        compiler_params=pltpu.CompilerParams(vmem_limit_bytes=limit * MIB),
        cost_estimate=pl.CostEstimate(flops=flops, bytes_accessed=size, transcendentals=0),
        **extra,
    )(*operands)


VMEM = pl.BlockSpec(memory_space=pltpu.VMEM)
HBM = pl.BlockSpec(memory_space=pltpu.HBM)


def shape_of(shape, dtype=BF):
    return jax.ShapeDtypeStruct(shape, dtype)


def one_hot(pos, tokens):
    hit = pos.astype(jnp.int32) == lane_ids((pos.shape[0], tokens))
    return jnp.where(hit, 1.0, 0.0).astype(BF)


def pick_kernel(token_ref, count_ref, gate_ref, resid_ref, out_ref, gain_ref, *sends):
    experts, capacity = token_ref.shape[1:]
    feat, tokens = resid_ref.shape[1:]
    lanes = sends[0].shape[1]
    slots = experts * capacity
    ep = lax.axis_index("ep")

    def column(ref):
        rows = []
        for s in range(experts):
            e = lax.rem(ep + s, experts)
            rows.append(jnp.broadcast_to(ref[0, pl.ds(e, 1), :], (capacity, capacity)))
        rows = jnp.concatenate(rows, axis=0)
        shape = (slots, capacity)
        mine = lane_ids(shape) == lax.rem(row_ids(shape), capacity)
        return jnp.sum(jnp.where(mine, rows.astype(F32), 0.0), axis=1, keepdims=True)

    counts = jnp.sum(
        jnp.where(
            lane_ids((slots, experts))
            == lax.rem(ep + row_ids((slots, experts)) // capacity, experts),
            jnp.broadcast_to(count_ref[...], (slots, experts)),
            0,
        ).astype(F32),
        axis=1,
        keepdims=True,
    )
    order = lax.rem(row_ids((slots, 1)), capacity).astype(F32)
    pos = jnp.where(order < counts, column(token_ref), -1.0)
    hot = one_hot(pos, tokens)
    picked = contract_cols(hot, resid_ref[0])
    grads = column(gate_ref) * contract_cols(hot, out_ref[0])
    gained = picked * gain_ref[...]
    for s in range(experts):
        rows = slice(s * capacity, (s + 1) * capacity)
        body = [picked[rows], grads[rows], gained[rows], gained[rows]]
        sends[s][:, :feat] = jnp.concatenate(body, axis=0).astype(BF)
        tail = jnp.concatenate([pos[rows]] * 4, axis=0)
        sends[s][:, feat:] = jnp.broadcast_to(tail, (4 * capacity, lanes - feat)).astype(BF)


def rows_of(blocks, feat):
    blocks = [b[...].astype(F32) for b in blocks]
    capacity = blocks[0].shape[0] // 4
    parts = [
        jnp.concatenate([b[k * capacity : (k + 1) * capacity, :feat] for b in blocks], axis=0)
        for k in range(3)
    ]
    pos = jnp.concatenate([b[:capacity, feat : feat + 1] for b in blocks], axis=0)
    return parts + [pos]


def fetch(sources, buffer, sems, steps):
    tile = buffer.shape[2] // steps
    copies = []
    for i in range(steps):
        part = slice(i * tile, (i + 1) * tile)
        row = []
        for n, source in enumerate(sources):
            row.append(
                pltpu.make_async_copy(
                    source.at[0, :, part], buffer.at[n, :, part], sems.at[n, i]
                )
            )
            row[-1].start()
        copies.append(row)
    return copies


def parts_kernel(features, groups, steps, *refs):
    got = refs[:groups]
    gate_ref, up_ref, down_ref, sums_ref, buffer, sems = refs[groups:]
    copies = fetch((gate_ref, up_ref, down_ref), buffer, sems, steps)
    feat = buffer.shape[1]
    count, _, lanes = sums_ref.shape
    unit = buffer.shape[2] // count
    chunk = count // steps
    tile = unit * chunk
    x, go, gained, _ = rows_of(got, feat)
    gained = gained.astype(BF)
    go = go.astype(BF)
    square = jnp.sum(x * x, axis=1, keepdims=True) / features
    tail = two_lanes(square, (x.shape[0], lanes - 3 * unit)).astype(BF)
    for i in range(steps):
        for n, rows in enumerate((gained, gained, go)):
            copies[i][n].wait()
            part = mm(rows, buffer[n, :, i * tile : (i + 1) * tile]).astype(BF)
            for k in range(chunk):
                u = i * chunk + k
                place = slice(n * unit, (n + 1) * unit)
                sums_ref[u, :, place] = part[:, k * unit : (k + 1) * unit]
        for k in range(chunk):
            u = i * chunk + k
            sums_ref[u, :, 3 * unit :] = tail


def activate(sums, unit):
    square = sums[:, 3 * unit : 3 * unit + 1] + sums[:, 3 * unit + 1 : 3 * unit + 2]
    inv_rms = lax.rsqrt(square + norm_eps)
    pre_gate = jnp.where(inv_rms > 0, sums[:, :unit] * inv_rms, 0.0)
    pre_up = jnp.where(inv_rms > 0, sums[:, unit : 2 * unit] * inv_rms, 0.0)
    hid_grad = sums[:, 2 * unit : 3 * unit]
    sigmoid_gate = 1.0 / (1.0 + jnp.exp(-pre_gate))
    silu_gate = pre_gate * sigmoid_gate
    hidden = (silu_gate * pre_up).astype(BF)
    d_gate = (hid_grad * pre_up * sigmoid_gate * (1.0 + pre_gate * (1.0 - sigmoid_gate))).astype(BF)
    d_up = (hid_grad * silu_gate).astype(BF)
    dots = jnp.sum(
        d_gate.astype(F32) * pre_gate + d_up.astype(F32) * pre_up, axis=1, keepdims=True
    )
    tail = two_lanes(dots, (sums.shape[0], sums.shape[1] - 3 * unit)).astype(BF)
    return inv_rms, jnp.concatenate([hidden, d_gate, d_up, tail], axis=1)


def act_kernel(unit, sums_ref, inv_ref, acts_ref):
    total = sums_ref[0].astype(F32)
    for k in range(1, sums_ref.shape[0]):
        total = total + sums_ref[k].astype(F32)
    inv_rms, acts = activate(total, unit)
    inv_ref[...] = jnp.broadcast_to(inv_rms, inv_ref.shape)
    for k in range(acts_ref.shape[0]):
        acts_ref[k] = acts


def delta_kernel(features, unit, groups, steps, *refs):
    got = refs[:groups]
    acts_ref, gain_ref, inv_ref, gate_ref, up_ref = refs[groups : groups + 5]
    hidden_ref, dgate_ref, dup_ref, slot_ref, go_ref, delta_ref = refs[groups + 5 : groups + 11]
    backs = refs[groups + 11 : 2 * groups + 11]
    buffer, sems = refs[2 * groups + 11 :]
    copies = fetch((gate_ref, up_ref), buffer, sems, steps)
    feat = buffer.shape[1]
    count = acts_ref.shape[0]
    chunk = count // steps
    tile = unit * chunk
    x, go, _, pos = rows_of(got, feat)
    inv_rms = inv_ref[:, :1]
    normed = x * inv_rms
    slot_ref[...] = (normed * gain_ref[:1]).astype(BF)
    go_ref[...] = go.astype(BF)
    dots = acts_ref[0, :, 3 * unit : 3 * unit + 128].astype(F32)
    for u in range(1, count):
        dots = dots + acts_ref[u, :, 3 * unit : 3 * unit + 128].astype(F32)
    dots = (dots[:, :1] + dots[:, 1:2]) / features
    total = jnp.zeros((x.shape[0], feat), F32)
    for i in range(steps):
        part = slice(i * tile, (i + 1) * tile)
        for n, ref in enumerate((hidden_ref, dgate_ref, dup_ref)):
            place = slice(n * unit, (n + 1) * unit)
            value = jnp.concatenate(
                [acts_ref[u, :, place] for u in range(i * chunk, (i + 1) * chunk)],
                axis=1,
            )
            ref[:, part] = value
            if n > 0:
                copies[i][n - 1].wait()
                total = total + contract_cols(value, buffer[n - 1, :, part])
    change = inv_rms * (total * gain_ref[:1] - normed * dots)
    tail = jnp.broadcast_to(pos, (pos.shape[0], delta_ref.shape[1] - feat))
    delta_ref[:, :feat] = change.astype(BF)
    delta_ref[:, feat:] = tail.astype(BF)
    capacity = backs[0].shape[0]
    for s in range(groups):
        rows = slice(s * capacity, (s + 1) * capacity)
        backs[s][:, :feat] = change[rows]
        backs[s][:, feat:] = tail[rows]


def grads_kernel(slot_ref, go_ref, hidden_ref, dgate_ref, dup_ref, gate_out, up_out, down_out):
    gate_out[0] = contract_rows(slot_ref[...], dgate_ref[...]).astype(BF)
    up_out[0] = contract_rows(slot_ref[...], dup_ref[...]).astype(BF)
    down_out[0] = contract_rows(go_ref[...], hidden_ref[...]).astype(BF)


def back_rows(backs, feat):
    rows = jnp.concatenate([b[...] for b in backs], axis=0)
    return rows[:, :feat].astype(BF), rows[:, feat : feat + 1]


def resid_kernel(*refs):
    out_ref, resid_ref = refs[-2:]
    feat, tokens = out_ref.shape[1:]
    change, pos = back_rows(refs[:-2], feat)
    change = contract_rows(change, one_hot(pos, tokens))
    resid_ref[0] = (out_ref[0].astype(F32) + change).astype(BF)


def plain_kernel(block_ref, w_ref, *refs):
    outs, acc_ref = refs[:-1], refs[-1]
    step = pl.program_id(0)
    groups, cores, feat, tokens = block_ref.shape
    ep = lax.axis_index("ep")

    @pl.when(step == 0)
    def _():
        acc_ref[...] = jnp.zeros_like(acc_ref)

    columns = []
    for shift in range(groups):
        g = lax.rem(ep + shift, groups)
        columns.append(jnp.concatenate([block_ref[g, c] for c in range(cores)], axis=0))
    acc_ref[...] += contract_rows(jnp.concatenate(columns, axis=1), w_ref[...])

    @pl.when(step == pl.num_programs(0) - 1)
    def _():
        for shift in range(groups):
            outs[shift][...] = acc_ref[shift * tokens : (shift + 1) * tokens, :].astype(BF)


def fixed_kernel(delta_ref, w_ref, *refs):
    outs, (acc_ref, buffer, sems) = refs[:-3], refs[-3:]
    experts, quarters, cores, rows, _ = delta_ref.shape
    groups = len(outs)
    capacity = rows // groups
    feat = w_ref.shape[0] // (quarters * cores)
    ep = lax.axis_index("ep")
    copies = []
    for j in range(quarters * cores):
        part = slice(j * feat, (j + 1) * feat)
        copies.append(pltpu.make_async_copy(w_ref.at[part, :], buffer.at[part, :], sems.at[j]))
        copies[-1].start()
    for j in range(quarters * cores):
        delta = [delta_ref[e, j // cores, j % cores] for e in range(experts)]
        delta = jnp.concatenate(delta, axis=0)[:, :feat]
        copies[j].wait()
        part = mm(delta, buffer[j * feat : (j + 1) * feat, :])
        acc_ref[...] = part if j == 0 else acc_ref[...] + part
    for shift in range(groups):
        pieces = []
        for s in range(experts):
            e = lax.rem(ep + shift + s, experts)
            start = pl.multiple_of(e * rows + s * capacity, 8)
            pieces.append(acc_ref[pl.ds(start, capacity), :])
        outs[shift][...] = jnp.concatenate(pieces, axis=0).astype(BF)


def weight_kernel(block_ref, delta_ref, ctx_ref, out_ref):
    groups, cores, feat, tokens = block_ref.shape
    experts, _, _, rows, _ = delta_ref.shape
    capacity = rows // groups
    ep = lax.axis_index("ep")
    columns = experts * rows
    row = row_ids((columns, 1))
    group_of = lax.rem(row // rows - lax.rem(row // capacity, groups) + groups, groups)
    order = [lax.rem(ep - shift + groups, groups) for shift in range(groups)]
    packed = jnp.concatenate([delta_ref[e, 0, 0] for e in range(experts)], axis=0)
    pos = packed[:, feat : feat + 1].astype(F32)
    hot = jnp.concatenate(
        [one_hot(jnp.where(group_of == g, pos, -1.0), tokens) for g in order], axis=1
    )
    blocks = []
    for c in range(cores):
        delta = jnp.concatenate([delta_ref[e, 0, c] for e in range(experts)], axis=0)[:, :feat]
        plain = jnp.concatenate([block_ref[g, c] for g in order], axis=1)
        blocks.append((plain.astype(F32) + contract_rows(delta, hot)).astype(BF))
    out_ref[...] = mm(jnp.concatenate(blocks, axis=0), ctx_ref[...]).astype(BF)


def context_kernel(groups, *refs):
    out_ref = refs[-1]
    tokens = out_ref.shape[2]
    backs, plains, fixes = refs[:groups], refs[groups : 2 * groups], refs[2 * groups : -1]
    pos = jnp.concatenate([b[:, b.shape[1] - 1 :] for b in backs], axis=0)
    total = plains[0][...].astype(F32)
    for ref in plains[1:]:
        total = total + ref[...].astype(F32)
    hot = one_hot(pos, tokens)
    for ref in fixes:
        total = total + contract_rows(hot, ref[...])
    out_ref[0] = total.T.astype(BF)


def shards(
    residual,
    out_grad,
    norm_gain,
    context,
    w_out,
    w_gate,
    w_up,
    w_down,
    slot_token,
    slot_count,
    slot_gate,
):
    tp_count = lax.axis_size("tp")
    ep_count = lax.axis_size("ep")
    near = tp_count // ep_count
    feat, tokens = residual.shape[1:]
    features = feat * tp_count
    experts, capacity = slot_token.shape[1:]
    groups = ep_count
    slots = experts * capacity
    rows = groups * capacity
    hidden_units = w_gate.shape[2]
    unit = hidden_units // tp_count
    atts = w_out.shape[1]
    lanes = -(-(feat + 1) // 128) * 128
    gain_row = norm_gain[None, :]
    ahead = [[(i, (i + s) % ep_count) for i in range(ep_count)] for s in range(ep_count)]
    behind = [[(i, (i - s) % ep_count) for i in range(ep_count)] for s in range(ep_count)]

    sends = call(
        pick_kernel,
        [shape_of((4 * capacity, lanes))] * experts,
        [slot_token, slot_count, slot_gate, residual, out_grad, norm_gain[None, :]],
        [VMEM] * 6,
        [VMEM] * experts,
        flops=4 * slots * tokens * feat,
        limit=56,
    )
    got = [sends[0]] + [lax.ppermute(sends[s], "ep", ahead[s]) for s in range(1, ep_count)]

    route = []
    for a in range(tp_count):
        for b in range(ep_count):
            route.append((a * ep_count + b, (b * near + a % near) * ep_count + a // near))
    moved = lax.ppermute(out_grad[0], ("tp", "ep"), route)

    steps = 4
    tile = hidden_units // steps
    wide = 3 * unit + 128
    if unit % 128 == 0:
        (sums,) = call(
            functools.partial(parts_kernel, features, groups, steps),
            [shape_of((tp_count, rows, wide))],
            got + [w_gate, w_up, w_down],
            [VMEM] * groups + [HBM] * 3,
            [VMEM],
            scratch=[
                pltpu.VMEM((3, feat, hidden_units), BF),
                pltpu.SemaphoreType.DMA((3, steps)),
            ],
            flops=6 * rows * feat * hidden_units,
        )
    else:
        x, go, gained, _ = rows_of(got, feat)
        gained = gained.astype(BF)
        square = jnp.sum(x * x, axis=1, keepdims=True) / features
        parts = [mm(gained, w_gate[0]), mm(gained, w_up[0]), mm(go.astype(BF), w_down[0])]
        parts = [p.astype(BF).reshape(rows, tp_count, unit).transpose(1, 0, 2) for p in parts]
        tail = two_lanes(square, (rows, 128)).astype(BF)
        tail = jnp.broadcast_to(tail[None], (tp_count, rows, 128))
        sums = jnp.concatenate(parts + [tail], axis=2)
    sums, moved = lax.optimization_barrier((sums, moved))
    block = lax.all_gather(moved, "tp", axis=0).reshape(groups, near, feat, tokens)
    sums = lax.all_to_all(sums, "tp", split_axis=0, concat_axis=0, tiled=True)
    if unit % 128 == 0:
        inv_rms, acts = call(
            functools.partial(act_kernel, unit),
            [shape_of((rows, 128), F32), shape_of((tp_count, rows, wide))],
            [sums],
            [VMEM],
            [VMEM, VMEM],
        )
    else:
        inv_rms, acts = activate(jnp.sum(sums.astype(F32), axis=0), unit)
        inv_rms = jnp.broadcast_to(inv_rms, (rows, 128))
        acts = jnp.broadcast_to(acts[None], (tp_count,) + acts.shape)
    acts, ctx_own = lax.optimization_barrier((acts, context[0]))
    acts = lax.all_to_all(acts, "tp", split_axis=0, concat_axis=0, tiled=True)

    ctx_own = ctx_own.T
    ctx_parts = [ctx_own] + [lax.ppermute(ctx_own, "ep", ahead[s]) for s in range(1, ep_count)]
    ctx_all = jnp.concatenate(ctx_parts, axis=0)
    acts, ctx_all = lax.optimization_barrier((acts, ctx_all))
    if unit % 128 == 0:
        made = call(
            functools.partial(delta_kernel, features, unit, groups, steps),
            [shape_of((rows, hidden_units))] * 3
            + [shape_of((rows, feat))] * 2
            + [shape_of((rows, lanes))]
            + [shape_of((capacity, lanes), F32)] * groups,
            got + [acts, gain_row, inv_rms, w_gate, w_up],
            [VMEM] * (groups + 3) + [HBM] * 2,
            [VMEM] * (6 + groups),
            scratch=[
                pltpu.VMEM((2, feat, hidden_units), BF),
                pltpu.SemaphoreType.DMA((2, steps)),
            ],
            flops=4 * rows * feat * hidden_units,
        )
        hidden, d_gate, d_up, slot_in, rows_go, delta = made[:6]
        backs = list(made[6:])
    else:
        x, go, _, pos = rows_of(got, feat)
        rows_go = go.astype(BF)
        hidden, d_gate, d_up = [
            acts[:, :, n * unit : (n + 1) * unit].transpose(1, 0, 2).reshape(rows, hidden_units)
            for n in range(3)
        ]
        dots = jnp.sum(acts[:, :, 3 * unit : 3 * unit + 2].astype(F32), axis=(0, 2))[:, None]
        normed = x * inv_rms[:, :1]
        slot_in = (normed * norm_gain[None, :]).astype(BF)
        slot_back = contract_cols(d_gate, w_gate[0]) + contract_cols(d_up, w_up[0])
        change = inv_rms[:, :1] * (slot_back * norm_gain[None, :] - normed * (dots / features))
        packed = jnp.concatenate([change, jnp.broadcast_to(pos, (rows, lanes - feat))], axis=1)
        delta = packed.astype(BF)
        backs = [packed[s * capacity : (s + 1) * capacity] for s in range(groups)]

    spread = lax.ppermute(delta, ("tp", "ep"), route)
    backs = [backs[0]] + [lax.ppermute(backs[s], "ep", behind[s]) for s in range(1, ep_count)]
    grads = call(
        grads_kernel,
        [shape_of((1, feat, hidden_units))] * 3,
        [slot_in, rows_go, hidden, d_gate, d_up],
        [pl.BlockSpec((rows, feat), lambda i: (0, 0))] * 2
        + [pl.BlockSpec((rows, tile), lambda i: (0, i))] * 3,
        [pl.BlockSpec((1, feat, tile), lambda i: (0, 0, i))] * 3,
        grid=(steps,),
        flops=6 * rows * feat * hidden_units,
    )
    spread, grads = lax.optimization_barrier((spread, grads))
    spread = jnp.broadcast_to(spread[None], (tp_count, rows, lanes))
    spread = lax.all_to_all(spread, "tp", split_axis=0, concat_axis=0, tiled=True)
    spread = spread.reshape(experts, near // 2, 2, rows, lanes)

    quarters = near // 2
    out_block = pl.BlockSpec((groups, 2, feat, tokens), lambda q: (0, q, 0, 0))
    delta_block = pl.BlockSpec((experts, 1, 2, rows, lanes), lambda q: (0, q, 0, 0, 0))
    w_block = pl.BlockSpec((2 * feat, atts), lambda q: (q, 0))
    plain = call(
        plain_kernel,
        [shape_of((tokens, atts))] * groups,
        [block, w_out],
        [out_block, w_block],
        [pl.BlockSpec((tokens, atts), lambda q: (0, 0))] * groups,
        grid=(quarters,),
        scratch=[pltpu.VMEM((groups * tokens, atts), F32)],
        flops=2 * groups * tokens * near * feat * atts,
        limit=52,
    )
    spread, plain = lax.optimization_barrier((spread, plain))
    plains = [plain[0]] + [lax.ppermute(plain[s], "ep", ahead[s]) for s in range(1, ep_count)]
    fixed = call(
        fixed_kernel,
        [shape_of((slots, atts))] * groups,
        [spread, w_out],
        [VMEM, HBM],
        [VMEM] * groups,
        scratch=[
            pltpu.VMEM((experts * rows, atts), F32),
            pltpu.VMEM(w_out.shape, BF),
            pltpu.SemaphoreType.DMA((near,)),
        ],
        flops=2 * experts * rows * near * feat * atts,
        limit=52,
    )
    spread, fixed = lax.optimization_barrier((spread, fixed))
    fixes = [fixed[0]] + [lax.ppermute(fixed[s], "ep", ahead[s]) for s in range(1, ep_count)]
    (w_out_grad,) = call(
        weight_kernel,
        [shape_of((near * feat, atts))],
        [block, spread, ctx_all],
        [out_block, delta_block, pl.BlockSpec(ctx_all.shape, lambda q: (0, 0))],
        [pl.BlockSpec((2 * feat, atts), lambda q: (q, 0))],
        grid=(quarters,),
        flops=2 * groups * tokens * near * feat * atts,
        limit=52,
    )
    (w_out_grad, backs) = lax.optimization_barrier((w_out_grad, backs))
    (resid,) = call(
        resid_kernel,
        [shape_of((1, feat, tokens))],
        backs + [out_grad],
        [VMEM] * (groups + 1),
        [VMEM],
        flops=2 * slots * feat * tokens,
    )
    (ctx_grad,) = call(
        functools.partial(context_kernel, groups),
        [shape_of((1, atts, tokens))],
        backs + plains + fixes,
        [VMEM] * (3 * groups),
        [VMEM],
        flops=2 * slots * tokens * atts,
    )
    return (resid, ctx_grad, w_out_grad) + tuple(grads)


def solution(mesh):
    return jax.shard_map(
        shards,
        mesh=mesh,
        in_specs=(
            P("ep", "tp", None),
            P("ep", "tp", None),
            P("tp"),
            P("ep", "tp", None),
            P("ep", "tp"),
            P("ep", "tp", None),
            P("ep", "tp", None),
            P("ep", "tp", None),
            P("ep", None, None),
            P("ep", None),
            P("ep", None, None),
        ),
        out_specs=(
            P("ep", "tp", None),
            P("ep", "tp", None),
            P("ep", "tp"),
            P("ep", "tp", None),
            P("ep", "tp", None),
            P("ep", "tp", None),
        ),
        check_vma=False,
    )
```

```python
import functools

import jax
import jax.numpy as jnp
from jax import lax
from jax.experimental import pallas as pl
from jax.experimental.pallas import tpu as pltpu
from jax.sharding import PartitionSpec as P

norm_eps = 1e-06
BF = jnp.bfloat16
F32 = jnp.float32
MIB = 1024 * 1024


def mm(left, right):
    return jnp.dot(left, right, preferred_element_type=F32)


def contract_rows(left, right):
    return lax.dot_general(left, right, (((0,), (0,)), ((), ())), preferred_element_type=F32)


def contract_cols(left, right):
    return lax.dot_general(left, right, (((1,), (1,)), ((), ())), preferred_element_type=F32)


def split_two(value):
    high = value.astype(BF).astype(F32)
    rest = jnp.where(jnp.abs(value) < jnp.inf, value - high, 0.0)
    return high, rest


def lane_ids(shape):
    return lax.broadcasted_iota(jnp.int32, shape, len(shape) - 1)


def row_ids(shape):
    return lax.broadcasted_iota(jnp.int32, shape, len(shape) - 2)


def two_lanes(value, shape):
    high, rest = split_two(value)
    lane = lane_ids(shape)
    return jnp.where(lane == 0, high, jnp.where(lane == 1, rest, 0.0))


def call(kernel, outs, operands, in_specs, out_specs, grid=None, scratch=(), flops=0, limit=52):
    size = 0
    for leaf in list(outs) + list(operands):
        count = 1
        for dim in leaf.shape:
            count *= dim
        size += count * leaf.dtype.itemsize
    extra = {} if grid is None else {"grid": grid}
    return pl.pallas_call(
        kernel,
        out_shape=tuple(outs),
        in_specs=in_specs,
        out_specs=tuple(out_specs),
        scratch_shapes=list(scratch),
        compiler_params=pltpu.CompilerParams(vmem_limit_bytes=limit * MIB),
        cost_estimate=pl.CostEstimate(flops=flops, bytes_accessed=size, transcendentals=0),
        **extra,
    )(*operands)


VMEM = pl.BlockSpec(memory_space=pltpu.VMEM)
HBM = pl.BlockSpec(memory_space=pltpu.HBM)


def shape_of(shape, dtype=BF):
    return jax.ShapeDtypeStruct(shape, dtype)


def one_hot(pos, tokens):
    hit = pos.astype(jnp.int32) == lane_ids((pos.shape[0], tokens))
    return jnp.where(hit, 1.0, 0.0).astype(BF)


def pick_kernel(token_ref, count_ref, gate_ref, resid_ref, out_ref, gain_ref, *sends):
    experts, capacity = token_ref.shape[1:]
    feat, tokens = resid_ref.shape[1:]
    lanes = sends[0].shape[1]
    slots = experts * capacity
    ep = lax.axis_index("ep")

    def column(ref):
        rows = []
        for s in range(experts):
            e = lax.rem(ep + s, experts)
            rows.append(jnp.broadcast_to(ref[0, pl.ds(e, 1), :], (capacity, capacity)))
        rows = jnp.concatenate(rows, axis=0)
        shape = (slots, capacity)
        mine = lane_ids(shape) == lax.rem(row_ids(shape), capacity)
        return jnp.sum(jnp.where(mine, rows.astype(F32), 0.0), axis=1, keepdims=True)

    counts = jnp.sum(
        jnp.where(
            lane_ids((slots, experts))
            == lax.rem(ep + row_ids((slots, experts)) // capacity, experts),
            jnp.broadcast_to(count_ref[...], (slots, experts)),
            0,
        ).astype(F32),
        axis=1,
        keepdims=True,
    )
    order = lax.rem(row_ids((slots, 1)), capacity).astype(F32)
    pos = jnp.where(order < counts, column(token_ref), -1.0)
    hot = one_hot(pos, tokens)
    picked = contract_cols(hot, resid_ref[0])
    grads = column(gate_ref) * contract_cols(hot, out_ref[0])
    gained = picked * gain_ref[...]
    for s in range(experts):
        rows = slice(s * capacity, (s + 1) * capacity)
        body = [picked[rows], grads[rows], gained[rows], gained[rows]]
        sends[s][:, :feat] = jnp.concatenate(body, axis=0).astype(BF)
        tail = jnp.concatenate([pos[rows]] * 4, axis=0)
        sends[s][:, feat:] = jnp.broadcast_to(tail, (4 * capacity, lanes - feat)).astype(BF)


def rows_of(blocks, feat):
    blocks = [b[...].astype(F32) for b in blocks]
    capacity = blocks[0].shape[0] // 4
    parts = [
        jnp.concatenate([b[k * capacity : (k + 1) * capacity, :feat] for b in blocks], axis=0)
        for k in range(3)
    ]
    pos = jnp.concatenate([b[:capacity, feat : feat + 1] for b in blocks], axis=0)
    return parts + [pos]


def fetch(sources, buffer, sems, steps):
    tile = buffer.shape[2] // steps
    copies = []
    for i in range(steps):
        part = slice(i * tile, (i + 1) * tile)
        row = []
        for n, source in enumerate(sources):
            row.append(
                pltpu.make_async_copy(
                    source.at[0, :, part], buffer.at[n, :, part], sems.at[n, i]
                )
            )
            row[-1].start()
        copies.append(row)
    return copies


def parts_kernel(features, groups, steps, *refs):
    got = refs[:groups]
    gate_ref, up_ref, down_ref, sums_ref, buffer, sems = refs[groups:]
    copies = fetch((gate_ref, up_ref, down_ref), buffer, sems, steps)
    feat = buffer.shape[1]
    count, _, lanes = sums_ref.shape
    unit = buffer.shape[2] // count
    chunk = count // steps
    tile = unit * chunk
    x, go, gained, _ = rows_of(got, feat)
    gained = gained.astype(BF)
    go = go.astype(BF)
    square = jnp.sum(x * x, axis=1, keepdims=True) / features
    tail = two_lanes(square, (x.shape[0], lanes - 3 * unit)).astype(BF)
    for i in range(steps):
        for n, rows in enumerate((gained, gained, go)):
            copies[i][n].wait()
            part = mm(rows, buffer[n, :, i * tile : (i + 1) * tile]).astype(BF)
            for k in range(chunk):
                u = i * chunk + k
                place = slice(n * unit, (n + 1) * unit)
                sums_ref[u, :, place] = part[:, k * unit : (k + 1) * unit]
        for k in range(chunk):
            u = i * chunk + k
            sums_ref[u, :, 3 * unit :] = tail


def activate(sums, unit):
    square = sums[:, 3 * unit : 3 * unit + 1] + sums[:, 3 * unit + 1 : 3 * unit + 2]
    inv_rms = lax.rsqrt(square + norm_eps)
    pre_gate = jnp.where(inv_rms > 0, sums[:, :unit] * inv_rms, 0.0)
    pre_up = jnp.where(inv_rms > 0, sums[:, unit : 2 * unit] * inv_rms, 0.0)
    hid_grad = sums[:, 2 * unit : 3 * unit]
    sigmoid_gate = 1.0 / (1.0 + jnp.exp(-pre_gate))
    silu_gate = pre_gate * sigmoid_gate
    hidden = (silu_gate * pre_up).astype(BF)
    d_gate = (hid_grad * pre_up * sigmoid_gate * (1.0 + pre_gate * (1.0 - sigmoid_gate))).astype(BF)
    d_up = (hid_grad * silu_gate).astype(BF)
    dots = jnp.sum(
        d_gate.astype(F32) * pre_gate + d_up.astype(F32) * pre_up, axis=1, keepdims=True
    )
    tail = two_lanes(dots, (sums.shape[0], sums.shape[1] - 3 * unit)).astype(BF)
    return inv_rms, jnp.concatenate([hidden, d_gate, d_up, tail], axis=1)


def act_kernel(unit, sums_ref, inv_ref, acts_ref):
    total = sums_ref[0].astype(F32)
    for k in range(1, sums_ref.shape[0]):
        total = total + sums_ref[k].astype(F32)
    inv_rms, acts = activate(total, unit)
    inv_ref[...] = jnp.broadcast_to(inv_rms, inv_ref.shape)
    for k in range(acts_ref.shape[0]):
        acts_ref[k] = acts


def delta_kernel(features, unit, groups, steps, *refs):
    got = refs[:groups]
    acts_ref, gain_ref, inv_ref, gate_ref, up_ref = refs[groups : groups + 5]
    hidden_ref, dgate_ref, dup_ref, slot_ref, go_ref, delta_ref = refs[groups + 5 : groups + 11]
    backs = refs[groups + 11 : 2 * groups + 11]
    buffer, sems = refs[2 * groups + 11 :]
    copies = fetch((gate_ref, up_ref), buffer, sems, steps)
    feat = buffer.shape[1]
    count = acts_ref.shape[0]
    chunk = count // steps
    tile = unit * chunk
    x, go, _, pos = rows_of(got, feat)
    inv_rms = inv_ref[:, :1]
    normed = x * inv_rms
    slot_ref[...] = (normed * gain_ref[:1]).astype(BF)
    go_ref[...] = go.astype(BF)
    dots = acts_ref[0, :, 3 * unit : 3 * unit + 128].astype(F32)
    for u in range(1, count):
        dots = dots + acts_ref[u, :, 3 * unit : 3 * unit + 128].astype(F32)
    dots = (dots[:, :1] + dots[:, 1:2]) / features
    total = jnp.zeros((x.shape[0], feat), F32)
    for i in range(steps):
        part = slice(i * tile, (i + 1) * tile)
        for n, ref in enumerate((hidden_ref, dgate_ref, dup_ref)):
            place = slice(n * unit, (n + 1) * unit)
            value = jnp.concatenate(
                [acts_ref[u, :, place] for u in range(i * chunk, (i + 1) * chunk)],
                axis=1,
            )
            ref[:, part] = value
            if n > 0:
                copies[i][n - 1].wait()
                total = total + contract_cols(value, buffer[n - 1, :, part])
    change = inv_rms * (total * gain_ref[:1] - normed * dots)
    tail = jnp.broadcast_to(pos, (pos.shape[0], delta_ref.shape[1] - feat))
    delta_ref[:, :feat] = change.astype(BF)
    delta_ref[:, feat:] = tail.astype(BF)
    capacity = backs[0].shape[0]
    for s in range(groups):
        rows = slice(s * capacity, (s + 1) * capacity)
        backs[s][:, :feat] = change[rows]
        backs[s][:, feat:] = tail[rows]


def grads_kernel(slot_ref, go_ref, hidden_ref, dgate_ref, dup_ref, gate_out, up_out, down_out):
    gate_out[0] = contract_rows(slot_ref[...], dgate_ref[...]).astype(BF)
    up_out[0] = contract_rows(slot_ref[...], dup_ref[...]).astype(BF)
    down_out[0] = contract_rows(go_ref[...], hidden_ref[...]).astype(BF)


def back_rows(backs, feat):
    rows = jnp.concatenate([b[...] for b in backs], axis=0)
    return rows[:, :feat].astype(BF), rows[:, feat : feat + 1]


def plain_kernel(block_ref, w_ref, *refs):
    outs, acc_ref = refs[:-1], refs[-1]
    step = pl.program_id(0)
    groups, cores, feat, tokens = block_ref.shape
    ep = lax.axis_index("ep")

    @pl.when(step == 0)
    def _():
        acc_ref[...] = jnp.zeros_like(acc_ref)

    columns = []
    for shift in range(groups):
        g = lax.rem(ep + shift, groups)
        columns.append(jnp.concatenate([block_ref[g, c] for c in range(cores)], axis=0))
    acc_ref[...] += contract_rows(jnp.concatenate(columns, axis=1), w_ref[...])

    @pl.when(step == pl.num_programs(0) - 1)
    def _():
        for shift in range(groups):
            outs[shift][...] = acc_ref[shift * tokens : (shift + 1) * tokens, :].astype(BF)


def fixed_kernel(delta_ref, w_ref, *refs):
    outs, (acc_ref, buffer, sems) = refs[:-3], refs[-3:]
    experts, quarters, cores, rows, _ = delta_ref.shape
    groups = len(outs)
    capacity = rows // groups
    feat = w_ref.shape[0] // (quarters * cores)
    ep = lax.axis_index("ep")
    copies = []
    for j in range(quarters * cores):
        part = slice(j * feat, (j + 1) * feat)
        copies.append(pltpu.make_async_copy(w_ref.at[part, :], buffer.at[part, :], sems.at[j]))
        copies[-1].start()
    for j in range(quarters * cores):
        delta = [delta_ref[e, j // cores, j % cores] for e in range(experts)]
        delta = jnp.concatenate(delta, axis=0)[:, :feat]
        copies[j].wait()
        part = mm(delta, buffer[j * feat : (j + 1) * feat, :])
        acc_ref[...] = part if j == 0 else acc_ref[...] + part
    for shift in range(groups):
        pieces = []
        for s in range(experts):
            e = lax.rem(ep + shift + s, experts)
            start = pl.multiple_of(e * rows + s * capacity, 8)
            pieces.append(acc_ref[pl.ds(start, capacity), :])
        outs[shift][...] = jnp.concatenate(pieces, axis=0).astype(BF)


def weight_kernel(block_ref, delta_ref, ctx_ref, out_ref):
    groups, cores, feat, tokens = block_ref.shape
    experts, _, _, rows, _ = delta_ref.shape
    capacity = rows // groups
    ep = lax.axis_index("ep")
    columns = experts * rows
    row = row_ids((columns, 1))
    group_of = lax.rem(row // rows - lax.rem(row // capacity, groups) + groups, groups)
    order = [lax.rem(ep - shift + groups, groups) for shift in range(groups)]
    packed = jnp.concatenate([delta_ref[e, 0, 0] for e in range(experts)], axis=0)
    pos = packed[:, feat : feat + 1].astype(F32)
    hot = jnp.concatenate(
        [one_hot(jnp.where(group_of == g, pos, -1.0), tokens) for g in order], axis=1
    )
    blocks = []
    for c in range(cores):
        delta = jnp.concatenate([delta_ref[e, 0, c] for e in range(experts)], axis=0)[:, :feat]
        plain = jnp.concatenate([block_ref[g, c] for g in order], axis=1)
        blocks.append((plain.astype(F32) + contract_rows(delta, hot)).astype(BF))
    out_ref[...] = mm(jnp.concatenate(blocks, axis=0), ctx_ref[...]).astype(BF)


def context_kernel(groups, *refs):
    grad_ref, resid_ref, out_ref = refs[-3:]
    tokens = out_ref.shape[2]
    backs, plains, fixes = refs[:groups], refs[groups : 2 * groups], refs[2 * groups : -3]
    change, pos = back_rows(backs, grad_ref.shape[1])
    hot = one_hot(pos, tokens)
    resid_ref[0] = (grad_ref[0].astype(F32) + contract_rows(change, hot)).astype(BF)
    total = plains[0][...].astype(F32)
    for ref in plains[1:]:
        total = total + ref[...].astype(F32)
    for ref in fixes:
        total = total + contract_rows(hot, ref[...])
    out_ref[0] = total.T.astype(BF)


def shards(
    residual,
    out_grad,
    norm_gain,
    context,
    w_out,
    w_gate,
    w_up,
    w_down,
    slot_token,
    slot_count,
    slot_gate,
):
    tp_count = lax.axis_size("tp")
    ep_count = lax.axis_size("ep")
    near = tp_count // ep_count
    feat, tokens = residual.shape[1:]
    features = feat * tp_count
    experts, capacity = slot_token.shape[1:]
    groups = ep_count
    slots = experts * capacity
    rows = groups * capacity
    hidden_units = w_gate.shape[2]
    unit = hidden_units // tp_count
    atts = w_out.shape[1]
    lanes = -(-(feat + 1) // 128) * 128
    gain_row = norm_gain[None, :]
    ahead = [[(i, (i + s) % ep_count) for i in range(ep_count)] for s in range(ep_count)]
    behind = [[(i, (i - s) % ep_count) for i in range(ep_count)] for s in range(ep_count)]

    sends = call(
        pick_kernel,
        [shape_of((4 * capacity, lanes))] * experts,
        [slot_token, slot_count, slot_gate, residual, out_grad, norm_gain[None, :]],
        [VMEM] * 6,
        [VMEM] * experts,
        flops=4 * slots * tokens * feat,
        limit=56,
    )
    got = [sends[0]] + [lax.ppermute(sends[s], "ep", ahead[s]) for s in range(1, ep_count)]

    route = []
    for a in range(tp_count):
        for b in range(ep_count):
            route.append((a * ep_count + b, (b * near + a % near) * ep_count + a // near))
    most = feat * 3 // 4 // 16 * 16
    early = lax.ppermute(out_grad[0, :most], ("tp", "ep"), route)
    rest, got = lax.optimization_barrier((out_grad[0, most:], got))
    rest = lax.ppermute(rest, ("tp", "ep"), route)

    steps = 4
    tile = hidden_units // steps
    wide = 3 * unit + 128
    if unit % 128 == 0:
        (sums,) = call(
            functools.partial(parts_kernel, features, groups, steps),
            [shape_of((tp_count, rows, wide))],
            got + [w_gate, w_up, w_down],
            [VMEM] * groups + [HBM] * 3,
            [VMEM],
            scratch=[
                pltpu.VMEM((3, feat, hidden_units), BF),
                pltpu.SemaphoreType.DMA((3, steps)),
            ],
            flops=6 * rows * feat * hidden_units,
        )
    else:
        x, go, gained, _ = rows_of(got, feat)
        gained = gained.astype(BF)
        square = jnp.sum(x * x, axis=1, keepdims=True) / features
        parts = [mm(gained, w_gate[0]), mm(gained, w_up[0]), mm(go.astype(BF), w_down[0])]
        parts = [p.astype(BF).reshape(rows, tp_count, unit).transpose(1, 0, 2) for p in parts]
        tail = two_lanes(square, (rows, 128)).astype(BF)
        tail = jnp.broadcast_to(tail[None], (tp_count, rows, 128))
        sums = jnp.concatenate(parts + [tail], axis=2)
    sums, early, rest = lax.optimization_barrier((sums, early, rest))
    moved = jnp.concatenate([early, rest], axis=0)
    block = lax.all_gather(moved, "tp", axis=0).reshape(groups, near, feat, tokens)
    sums = lax.all_to_all(sums, "tp", split_axis=0, concat_axis=0, tiled=True)
    if unit % 128 == 0:
        inv_rms, acts = call(
            functools.partial(act_kernel, unit),
            [shape_of((rows, 128), F32), shape_of((tp_count, rows, wide))],
            [sums],
            [VMEM],
            [VMEM, VMEM],
        )
    else:
        inv_rms, acts = activate(jnp.sum(sums.astype(F32), axis=0), unit)
        inv_rms = jnp.broadcast_to(inv_rms, (rows, 128))
        acts = jnp.broadcast_to(acts[None], (tp_count,) + acts.shape)
    acts, ctx_own = lax.optimization_barrier((acts, context[0]))
    acts = lax.all_to_all(acts, "tp", split_axis=0, concat_axis=0, tiled=True)

    ctx_own = ctx_own.T
    ctx_parts = [ctx_own] + [lax.ppermute(ctx_own, "ep", ahead[s]) for s in range(1, ep_count)]
    ctx_all = jnp.concatenate(ctx_parts, axis=0)
    acts, ctx_all = lax.optimization_barrier((acts, ctx_all))
    if unit % 128 == 0:
        made = call(
            functools.partial(delta_kernel, features, unit, groups, steps),
            [shape_of((rows, hidden_units))] * 3
            + [shape_of((rows, feat))] * 2
            + [shape_of((rows, lanes))]
            + [shape_of((capacity, lanes), F32)] * groups,
            got + [acts, gain_row, inv_rms, w_gate, w_up],
            [VMEM] * (groups + 3) + [HBM] * 2,
            [VMEM] * (6 + groups),
            scratch=[
                pltpu.VMEM((2, feat, hidden_units), BF),
                pltpu.SemaphoreType.DMA((2, steps)),
            ],
            flops=4 * rows * feat * hidden_units,
        )
        hidden, d_gate, d_up, slot_in, rows_go, delta = made[:6]
        backs = list(made[6:])
    else:
        x, go, _, pos = rows_of(got, feat)
        rows_go = go.astype(BF)
        hidden, d_gate, d_up = [
            acts[:, :, n * unit : (n + 1) * unit].transpose(1, 0, 2).reshape(rows, hidden_units)
            for n in range(3)
        ]
        dots = jnp.sum(acts[:, :, 3 * unit : 3 * unit + 2].astype(F32), axis=(0, 2))[:, None]
        normed = x * inv_rms[:, :1]
        slot_in = (normed * norm_gain[None, :]).astype(BF)
        slot_back = contract_cols(d_gate, w_gate[0]) + contract_cols(d_up, w_up[0])
        change = inv_rms[:, :1] * (slot_back * norm_gain[None, :] - normed * (dots / features))
        packed = jnp.concatenate([change, jnp.broadcast_to(pos, (rows, lanes - feat))], axis=1)
        delta = packed.astype(BF)
        backs = [packed[s * capacity : (s + 1) * capacity] for s in range(groups)]

    spread = lax.ppermute(delta, ("tp", "ep"), route)
    backs = [backs[0]] + [lax.ppermute(backs[s], "ep", behind[s]) for s in range(1, ep_count)]
    grads = call(
        grads_kernel,
        [shape_of((1, feat, hidden_units))] * 3,
        [slot_in, rows_go, hidden, d_gate, d_up],
        [pl.BlockSpec((rows, feat), lambda i: (0, 0))] * 2
        + [pl.BlockSpec((rows, tile), lambda i: (0, i))] * 3,
        [pl.BlockSpec((1, feat, tile), lambda i: (0, 0, i))] * 3,
        grid=(steps,),
        flops=6 * rows * feat * hidden_units,
    )
    spread, grads = lax.optimization_barrier((spread, grads))
    spread = jnp.broadcast_to(spread[None], (tp_count, rows, lanes))
    spread = lax.all_to_all(spread, "tp", split_axis=0, concat_axis=0, tiled=True)
    spread = spread.reshape(experts, near // 2, 2, rows, lanes)

    quarters = near // 2
    out_block = pl.BlockSpec((groups, 2, feat, tokens), lambda q: (0, q, 0, 0))
    delta_block = pl.BlockSpec((experts, 1, 2, rows, lanes), lambda q: (0, q, 0, 0, 0))
    w_block = pl.BlockSpec((2 * feat, atts), lambda q: (q, 0))
    plain = call(
        plain_kernel,
        [shape_of((tokens, atts))] * groups,
        [block, w_out],
        [out_block, w_block],
        [pl.BlockSpec((tokens, atts), lambda q: (0, 0))] * groups,
        grid=(quarters,),
        scratch=[pltpu.VMEM((groups * tokens, atts), F32)],
        flops=2 * groups * tokens * near * feat * atts,
        limit=52,
    )
    spread, plain = lax.optimization_barrier((spread, plain))
    plains = [plain[0]] + [lax.ppermute(plain[s], "ep", ahead[s]) for s in range(1, ep_count)]
    fixed = call(
        fixed_kernel,
        [shape_of((slots, atts))] * groups,
        [spread, w_out],
        [VMEM, HBM],
        [VMEM] * groups,
        scratch=[
            pltpu.VMEM((experts * rows, atts), F32),
            pltpu.VMEM(w_out.shape, BF),
            pltpu.SemaphoreType.DMA((near,)),
        ],
        flops=2 * experts * rows * near * feat * atts,
        limit=52,
    )
    spread, fixed = lax.optimization_barrier((spread, fixed))
    fixes = [fixed[0]] + [lax.ppermute(fixed[s], "ep", ahead[s]) for s in range(1, ep_count)]
    (w_out_grad,) = call(
        weight_kernel,
        [shape_of((near * feat, atts))],
        [block, spread, ctx_all],
        [out_block, delta_block, pl.BlockSpec(ctx_all.shape, lambda q: (0, 0))],
        [pl.BlockSpec((2 * feat, atts), lambda q: (q, 0))],
        grid=(quarters,),
        flops=2 * groups * tokens * near * feat * atts,
        limit=52,
    )
    resid, ctx_grad = call(
        functools.partial(context_kernel, groups),
        [shape_of((1, feat, tokens)), shape_of((1, atts, tokens))],
        backs + plains + fixes + [out_grad],
        [VMEM] * (3 * groups + 1),
        [VMEM] * 2,
        flops=2 * slots * tokens * (atts + feat),
    )
    return (resid, ctx_grad, w_out_grad) + tuple(grads)


def solution(mesh):
    return jax.shard_map(
        shards,
        mesh=mesh,
        in_specs=(
            P("ep", "tp", None),
            P("ep", "tp", None),
            P("tp"),
            P("ep", "tp", None),
            P("ep", "tp"),
            P("ep", "tp", None),
            P("ep", "tp", None),
            P("ep", "tp", None),
            P("ep", None, None),
            P("ep", None),
            P("ep", None, None),
        ),
        out_specs=(
            P("ep", "tp", None),
            P("ep", "tp", None),
            P("ep", "tp"),
            P("ep", "tp", None),
            P("ep", "tp", None),
            P("ep", "tp", None),
        ),
        check_vma=False,
    )
```

```python
import functools

import jax
import jax.numpy as jnp
from jax import lax
from jax.experimental import pallas as pl
from jax.experimental.pallas import tpu as pltpu
from jax.sharding import PartitionSpec as P

norm_eps = 1e-06
BF = jnp.bfloat16
F32 = jnp.float32
MIB = 1024 * 1024


def mm(left, right):
    return jnp.dot(left, right, preferred_element_type=F32)


def contract_rows(left, right):
    return lax.dot_general(left, right, (((0,), (0,)), ((), ())), preferred_element_type=F32)


def contract_cols(left, right):
    return lax.dot_general(left, right, (((1,), (1,)), ((), ())), preferred_element_type=F32)


def split_two(value):
    high = value.astype(BF).astype(F32)
    rest = jnp.where(jnp.abs(value) < jnp.inf, value - high, 0.0)
    return high, rest


def lane_ids(shape):
    return lax.broadcasted_iota(jnp.int32, shape, len(shape) - 1)


def row_ids(shape):
    return lax.broadcasted_iota(jnp.int32, shape, len(shape) - 2)


def two_lanes(value, shape):
    high, rest = split_two(value)
    lane = lane_ids(shape)
    return jnp.where(lane == 0, high, jnp.where(lane == 1, rest, 0.0))


def call(kernel, outs, operands, in_specs, out_specs, grid=None, scratch=(), flops=0, limit=52):
    size = 0
    for leaf in list(outs) + list(operands):
        count = 1
        for dim in leaf.shape:
            count *= dim
        size += count * leaf.dtype.itemsize
    extra = {} if grid is None else {"grid": grid}
    return pl.pallas_call(
        kernel,
        out_shape=tuple(outs),
        in_specs=in_specs,
        out_specs=tuple(out_specs),
        scratch_shapes=list(scratch),
        compiler_params=pltpu.CompilerParams(vmem_limit_bytes=limit * MIB),
        cost_estimate=pl.CostEstimate(flops=flops, bytes_accessed=size, transcendentals=0),
        **extra,
    )(*operands)


VMEM = pl.BlockSpec(memory_space=pltpu.VMEM)
HBM = pl.BlockSpec(memory_space=pltpu.HBM)


def shape_of(shape, dtype=BF):
    return jax.ShapeDtypeStruct(shape, dtype)


def one_hot(pos, tokens):
    hit = pos.astype(jnp.int32) == lane_ids((pos.shape[0], tokens))
    return jnp.where(hit, 1.0, 0.0).astype(BF)


def pick_kernel(token_ref, count_ref, gate_ref, resid_ref, out_ref, gain_ref, *sends):
    experts, capacity = token_ref.shape[1:]
    feat, tokens = resid_ref.shape[1:]
    lanes = sends[0].shape[1]
    slots = experts * capacity
    ep = lax.axis_index("ep")

    def column(ref):
        rows = []
        for s in range(experts):
            e = lax.rem(ep + s, experts)
            rows.append(jnp.broadcast_to(ref[0, pl.ds(e, 1), :], (capacity, capacity)))
        rows = jnp.concatenate(rows, axis=0)
        shape = (slots, capacity)
        mine = lane_ids(shape) == lax.rem(row_ids(shape), capacity)
        return jnp.sum(jnp.where(mine, rows.astype(F32), 0.0), axis=1, keepdims=True)

    counts = jnp.sum(
        jnp.where(
            lane_ids((slots, experts))
            == lax.rem(ep + row_ids((slots, experts)) // capacity, experts),
            jnp.broadcast_to(count_ref[...], (slots, experts)),
            0,
        ).astype(F32),
        axis=1,
        keepdims=True,
    )
    order = lax.rem(row_ids((slots, 1)), capacity).astype(F32)
    pos = jnp.where(order < counts, column(token_ref), -1.0)
    hot = one_hot(pos, tokens)
    picked = contract_cols(hot, resid_ref[0])
    grads = column(gate_ref) * contract_cols(hot, out_ref[0])
    gained = picked * gain_ref[...]
    for s in range(experts):
        rows = slice(s * capacity, (s + 1) * capacity)
        body = [picked[rows], grads[rows], gained[rows], gained[rows]]
        sends[s][:, :feat] = jnp.concatenate(body, axis=0).astype(BF)
        tail = jnp.concatenate([pos[rows]] * 4, axis=0)
        sends[s][:, feat:] = jnp.broadcast_to(tail, (4 * capacity, lanes - feat)).astype(BF)


def rows_of(blocks, feat):
    blocks = [b[...].astype(F32) for b in blocks]
    capacity = blocks[0].shape[0] // 4
    parts = [
        jnp.concatenate([b[k * capacity : (k + 1) * capacity, :feat] for b in blocks], axis=0)
        for k in range(3)
    ]
    pos = jnp.concatenate([b[:capacity, feat : feat + 1] for b in blocks], axis=0)
    return parts + [pos]


def fetch(sources, buffer, sems, steps):
    tile = buffer.shape[2] // steps
    copies = []
    for i in range(steps):
        part = slice(i * tile, (i + 1) * tile)
        row = []
        for n, source in enumerate(sources):
            row.append(
                pltpu.make_async_copy(
                    source.at[0, :, part], buffer.at[n, :, part], sems.at[n, i]
                )
            )
            row[-1].start()
        copies.append(row)
    return copies


def parts_kernel(features, groups, steps, *refs):
    got = refs[:groups]
    gate_ref, up_ref, down_ref, sums_ref, buffer, sems = refs[groups:]
    copies = fetch((gate_ref, up_ref, down_ref), buffer, sems, steps)
    feat = buffer.shape[1]
    count, _, lanes = sums_ref.shape
    unit = buffer.shape[2] // count
    chunk = count // steps
    tile = unit * chunk
    x, go, gained, _ = rows_of(got, feat)
    gained = gained.astype(BF)
    go = go.astype(BF)
    square = jnp.sum(x * x, axis=1, keepdims=True) / features
    tail = two_lanes(square, (x.shape[0], lanes - 3 * unit)).astype(BF)
    for i in range(steps):
        for n, rows in enumerate((gained, gained, go)):
            copies[i][n].wait()
            part = mm(rows, buffer[n, :, i * tile : (i + 1) * tile]).astype(BF)
            for k in range(chunk):
                u = i * chunk + k
                place = slice(n * unit, (n + 1) * unit)
                sums_ref[u, :, place] = part[:, k * unit : (k + 1) * unit]
        for k in range(chunk):
            u = i * chunk + k
            sums_ref[u, :, 3 * unit :] = tail


def activate(sums, unit):
    square = sums[:, 3 * unit : 3 * unit + 1] + sums[:, 3 * unit + 1 : 3 * unit + 2]
    inv_rms = lax.rsqrt(square + norm_eps)
    pre_gate = jnp.where(inv_rms > 0, sums[:, :unit] * inv_rms, 0.0)
    pre_up = jnp.where(inv_rms > 0, sums[:, unit : 2 * unit] * inv_rms, 0.0)
    hid_grad = sums[:, 2 * unit : 3 * unit]
    sigmoid_gate = 1.0 / (1.0 + jnp.exp(-pre_gate))
    silu_gate = pre_gate * sigmoid_gate
    hidden = (silu_gate * pre_up).astype(BF)
    d_gate = (hid_grad * pre_up * sigmoid_gate * (1.0 + pre_gate * (1.0 - sigmoid_gate))).astype(BF)
    d_up = (hid_grad * silu_gate).astype(BF)
    dots = jnp.sum(
        d_gate.astype(F32) * pre_gate + d_up.astype(F32) * pre_up, axis=1, keepdims=True
    )
    tail = two_lanes(dots, (sums.shape[0], sums.shape[1] - 3 * unit)).astype(BF)
    return inv_rms, jnp.concatenate([hidden, d_gate, d_up, tail], axis=1)


def act_kernel(unit, sums_ref, inv_ref, acts_ref):
    total = sums_ref[0].astype(F32)
    for k in range(1, sums_ref.shape[0]):
        total = total + sums_ref[k].astype(F32)
    inv_rms, acts = activate(total, unit)
    inv_ref[...] = jnp.broadcast_to(inv_rms, inv_ref.shape)
    for k in range(acts_ref.shape[0]):
        acts_ref[k] = acts


def delta_kernel(features, unit, groups, steps, *refs):
    got = refs[:groups]
    acts_ref, gain_ref, inv_ref, gate_ref, up_ref = refs[groups : groups + 5]
    hidden_ref, dgate_ref, dup_ref, slot_ref, go_ref, delta_ref = refs[groups + 5 : groups + 11]
    backs = refs[groups + 11 : 2 * groups + 11]
    buffer, sems = refs[2 * groups + 11 :]
    copies = fetch((gate_ref, up_ref), buffer, sems, steps)
    feat = buffer.shape[1]
    count = acts_ref.shape[0]
    chunk = count // steps
    tile = unit * chunk
    x, go, _, pos = rows_of(got, feat)
    inv_rms = inv_ref[:, :1]
    normed = x * inv_rms
    slot_ref[...] = (normed * gain_ref[:1]).astype(BF)
    go_ref[...] = go.astype(BF)
    dots = acts_ref[0, :, 3 * unit : 3 * unit + 128].astype(F32)
    for u in range(1, count):
        dots = dots + acts_ref[u, :, 3 * unit : 3 * unit + 128].astype(F32)
    dots = (dots[:, :1] + dots[:, 1:2]) / features
    total = jnp.zeros((x.shape[0], feat), F32)
    for i in range(steps):
        part = slice(i * tile, (i + 1) * tile)
        for n, ref in enumerate((hidden_ref, dgate_ref, dup_ref)):
            place = slice(n * unit, (n + 1) * unit)
            value = jnp.concatenate(
                [acts_ref[u, :, place] for u in range(i * chunk, (i + 1) * chunk)],
                axis=1,
            )
            ref[:, part] = value
            if n > 0:
                copies[i][n - 1].wait()
                total = total + contract_cols(value, buffer[n - 1, :, part])
    change = inv_rms * (total * gain_ref[:1] - normed * dots)
    tail = jnp.broadcast_to(pos, (pos.shape[0], delta_ref.shape[1] - feat))
    delta_ref[:, :feat] = change.astype(BF)
    delta_ref[:, feat:] = tail.astype(BF)
    capacity = backs[0].shape[0]
    for s in range(groups):
        rows = slice(s * capacity, (s + 1) * capacity)
        backs[s][:, :feat] = change[rows]
        backs[s][:, feat:] = tail[rows]


def grads_kernel(slot_ref, go_ref, hidden_ref, dgate_ref, dup_ref, gate_out, up_out, down_out):
    gate_out[0] = contract_rows(slot_ref[...], dgate_ref[...]).astype(BF)
    up_out[0] = contract_rows(slot_ref[...], dup_ref[...]).astype(BF)
    down_out[0] = contract_rows(go_ref[...], hidden_ref[...]).astype(BF)


def back_rows(backs, feat):
    rows = jnp.concatenate([b[...] for b in backs], axis=0)
    return rows[:, :feat].astype(BF), rows[:, feat : feat + 1]


def plain_kernel(block_ref, w_ref, *refs):
    outs, acc_ref = refs[:-1], refs[-1]
    step = pl.program_id(0)
    groups, cores, feat, tokens = block_ref.shape
    ep = lax.axis_index("ep")

    @pl.when(step == 0)
    def _():
        acc_ref[...] = jnp.zeros_like(acc_ref)

    columns = []
    for shift in range(groups):
        g = lax.rem(ep + shift, groups)
        columns.append(jnp.concatenate([block_ref[g, c] for c in range(cores)], axis=0))
    acc_ref[...] += contract_rows(jnp.concatenate(columns, axis=1), w_ref[...])

    @pl.when(step == pl.num_programs(0) - 1)
    def _():
        for shift in range(groups):
            outs[shift][...] = acc_ref[shift * tokens : (shift + 1) * tokens, :].astype(BF)


def fixed_kernel(delta_ref, w_ref, *refs):
    outs, (acc_ref, buffer, sems) = refs[:-3], refs[-3:]
    experts, quarters, cores, rows, _ = delta_ref.shape
    groups = len(outs)
    capacity = rows // groups
    feat = w_ref.shape[0] // (quarters * cores)
    ep = lax.axis_index("ep")
    copies = []
    for j in range(quarters * cores):
        part = slice(j * feat, (j + 1) * feat)
        copies.append(pltpu.make_async_copy(w_ref.at[part, :], buffer.at[part, :], sems.at[j]))
        copies[-1].start()
    for j in range(quarters * cores):
        delta = [delta_ref[e, j // cores, j % cores] for e in range(experts)]
        delta = jnp.concatenate(delta, axis=0)[:, :feat]
        copies[j].wait()
        part = mm(delta, buffer[j * feat : (j + 1) * feat, :])
        acc_ref[...] = part if j == 0 else acc_ref[...] + part
    for shift in range(groups):
        pieces = []
        for s in range(experts):
            e = lax.rem(ep + shift + s, experts)
            start = pl.multiple_of(e * rows + s * capacity, 8)
            pieces.append(acc_ref[pl.ds(start, capacity), :])
        outs[shift][...] = jnp.concatenate(pieces, axis=0).astype(BF)


def weight_kernel(block_ref, delta_ref, ctx_ref, out_ref):
    groups, cores, feat, tokens = block_ref.shape
    experts, _, _, rows, _ = delta_ref.shape
    capacity = rows // groups
    ep = lax.axis_index("ep")
    columns = experts * rows
    row = row_ids((columns, 1))
    group_of = lax.rem(row // rows - lax.rem(row // capacity, groups) + groups, groups)
    order = [lax.rem(ep - shift + groups, groups) for shift in range(groups)]
    packed = jnp.concatenate([delta_ref[e, 0, 0] for e in range(experts)], axis=0)
    pos = packed[:, feat : feat + 1].astype(F32)
    hot = jnp.concatenate(
        [one_hot(jnp.where(group_of == g, pos, -1.0), tokens) for g in order], axis=1
    )
    blocks = []
    for c in range(cores):
        delta = jnp.concatenate([delta_ref[e, 0, c] for e in range(experts)], axis=0)[:, :feat]
        plain = jnp.concatenate([block_ref[g, c] for g in order], axis=1)
        blocks.append((plain.astype(F32) + contract_rows(delta, hot)).astype(BF))
    out_ref[...] = mm(jnp.concatenate(blocks, axis=0), ctx_ref[...]).astype(BF)


def context_kernel(groups, *refs):
    grad_ref, resid_ref, out_ref = refs[-3:]
    tokens = out_ref.shape[2]
    backs, plains, fixes = refs[:groups], refs[groups : 2 * groups], refs[2 * groups : -3]
    change, pos = back_rows(backs, grad_ref.shape[1])
    hot = one_hot(pos, tokens)
    resid_ref[0] = (grad_ref[0].astype(F32) + contract_rows(change, hot)).astype(BF)
    total = plains[0][...].astype(F32)
    for ref in plains[1:]:
        total = total + ref[...].astype(F32)
    for ref in fixes:
        total = total + contract_rows(hot, ref[...])
    out_ref[0] = total.T.astype(BF)


def shards(
    residual,
    out_grad,
    norm_gain,
    context,
    w_out,
    w_gate,
    w_up,
    w_down,
    slot_token,
    slot_count,
    slot_gate,
):
    tp_count = lax.axis_size("tp")
    ep_count = lax.axis_size("ep")
    near = tp_count // ep_count
    feat, tokens = residual.shape[1:]
    features = feat * tp_count
    experts, capacity = slot_token.shape[1:]
    groups = ep_count
    slots = experts * capacity
    rows = groups * capacity
    hidden_units = w_gate.shape[2]
    unit = hidden_units // tp_count
    atts = w_out.shape[1]
    lanes = -(-(feat + 1) // 128) * 128
    gain_row = norm_gain[None, :]
    ahead = [[(i, (i + s) % ep_count) for i in range(ep_count)] for s in range(ep_count)]
    behind = [[(i, (i - s) % ep_count) for i in range(ep_count)] for s in range(ep_count)]

    sends = call(
        pick_kernel,
        [shape_of((4 * capacity, lanes))] * experts,
        [slot_token, slot_count, slot_gate, residual, out_grad, norm_gain[None, :]],
        [VMEM] * 6,
        [VMEM] * experts,
        flops=4 * slots * tokens * feat,
        limit=56,
    )
    got = [sends[0]] + [lax.ppermute(sends[s], "ep", ahead[s]) for s in range(1, ep_count)]

    route = []
    for a in range(tp_count):
        for b in range(ep_count):
            route.append((a * ep_count + b, (b * near + a % near) * ep_count + a // near))
    moved = lax.ppermute(out_grad[0], ("tp", "ep"), route)

    steps = 4
    tile = hidden_units // steps
    wide = 3 * unit + 128
    if unit % 128 == 0:
        (sums,) = call(
            functools.partial(parts_kernel, features, groups, steps),
            [shape_of((tp_count, rows, wide))],
            got + [w_gate, w_up, w_down],
            [VMEM] * groups + [HBM] * 3,
            [VMEM],
            scratch=[
                pltpu.VMEM((3, feat, hidden_units), BF),
                pltpu.SemaphoreType.DMA((3, steps)),
            ],
            flops=6 * rows * feat * hidden_units,
        )
    else:
        x, go, gained, _ = rows_of(got, feat)
        gained = gained.astype(BF)
        square = jnp.sum(x * x, axis=1, keepdims=True) / features
        parts = [mm(gained, w_gate[0]), mm(gained, w_up[0]), mm(go.astype(BF), w_down[0])]
        parts = [p.astype(BF).reshape(rows, tp_count, unit).transpose(1, 0, 2) for p in parts]
        tail = two_lanes(square, (rows, 128)).astype(BF)
        tail = jnp.broadcast_to(tail[None], (tp_count, rows, 128))
        sums = jnp.concatenate(parts + [tail], axis=2)
    sums, moved = lax.optimization_barrier((sums, moved))
    block = lax.all_gather(moved, "tp", axis=0).reshape(groups, near, feat, tokens)
    sums = lax.all_to_all(sums, "tp", split_axis=0, concat_axis=0, tiled=True)
    if unit % 128 == 0:
        inv_rms, acts = call(
            functools.partial(act_kernel, unit),
            [shape_of((rows, 128), F32), shape_of((tp_count, rows, wide))],
            [sums],
            [VMEM],
            [VMEM, VMEM],
        )
    else:
        inv_rms, acts = activate(jnp.sum(sums.astype(F32), axis=0), unit)
        inv_rms = jnp.broadcast_to(inv_rms, (rows, 128))
        acts = jnp.broadcast_to(acts[None], (tp_count,) + acts.shape)
    acts, ctx_own = lax.optimization_barrier((acts, context[0]))
    acts = lax.all_to_all(acts, "tp", split_axis=0, concat_axis=0, tiled=True)

    ctx_own = ctx_own.T
    ctx_parts = [ctx_own] + [lax.ppermute(ctx_own, "ep", ahead[s]) for s in range(1, ep_count)]
    ctx_all = jnp.concatenate(ctx_parts, axis=0)
    acts, ctx_all = lax.optimization_barrier((acts, ctx_all))
    if unit % 128 == 0:
        made = call(
            functools.partial(delta_kernel, features, unit, groups, steps),
            [shape_of((rows, hidden_units))] * 3
            + [shape_of((rows, feat))] * 2
            + [shape_of((rows, lanes))]
            + [shape_of((capacity, lanes), F32)] * groups,
            got + [acts, gain_row, inv_rms, w_gate, w_up],
            [VMEM] * (groups + 3) + [HBM] * 2,
            [VMEM] * (6 + groups),
            scratch=[
                pltpu.VMEM((2, feat, hidden_units), BF),
                pltpu.SemaphoreType.DMA((2, steps)),
            ],
            flops=4 * rows * feat * hidden_units,
        )
        hidden, d_gate, d_up, slot_in, rows_go, delta = made[:6]
        backs = list(made[6:])
    else:
        x, go, _, pos = rows_of(got, feat)
        rows_go = go.astype(BF)
        hidden, d_gate, d_up = [
            acts[:, :, n * unit : (n + 1) * unit].transpose(1, 0, 2).reshape(rows, hidden_units)
            for n in range(3)
        ]
        dots = jnp.sum(acts[:, :, 3 * unit : 3 * unit + 2].astype(F32), axis=(0, 2))[:, None]
        normed = x * inv_rms[:, :1]
        slot_in = (normed * norm_gain[None, :]).astype(BF)
        slot_back = contract_cols(d_gate, w_gate[0]) + contract_cols(d_up, w_up[0])
        change = inv_rms[:, :1] * (slot_back * norm_gain[None, :] - normed * (dots / features))
        packed = jnp.concatenate([change, jnp.broadcast_to(pos, (rows, lanes - feat))], axis=1)
        delta = packed.astype(BF)
        backs = [packed[s * capacity : (s + 1) * capacity] for s in range(groups)]

    spread = lax.ppermute(delta, ("tp", "ep"), route)
    backs = [backs[0]] + [lax.ppermute(backs[s], "ep", behind[s]) for s in range(1, ep_count)]
    grads = call(
        grads_kernel,
        [shape_of((1, feat, hidden_units))] * 3,
        [slot_in, rows_go, hidden, d_gate, d_up],
        [pl.BlockSpec((rows, feat), lambda i: (0, 0))] * 2
        + [pl.BlockSpec((rows, tile // 2), lambda i: (0, i))] * 3,
        [pl.BlockSpec((1, feat, tile // 2), lambda i: (0, 0, i))] * 3,
        grid=(2 * steps,),
        flops=6 * rows * feat * hidden_units,
    )
    spread, grads = lax.optimization_barrier((spread, grads))
    spread = jnp.broadcast_to(spread[None], (tp_count, rows, lanes))
    spread = lax.all_to_all(spread, "tp", split_axis=0, concat_axis=0, tiled=True)
    spread = spread.reshape(experts, near // 2, 2, rows, lanes)

    quarters = near // 2
    out_block = pl.BlockSpec((groups, 2, feat, tokens), lambda q: (0, q, 0, 0))
    w_block = pl.BlockSpec((2 * feat, atts), lambda q: (q, 0))
    plain = call(
        plain_kernel,
        [shape_of((tokens, atts))] * groups,
        [block, w_out],
        [out_block, w_block],
        [pl.BlockSpec((tokens, atts), lambda q: (0, 0))] * groups,
        grid=(quarters,),
        scratch=[pltpu.VMEM((groups * tokens, atts), F32)],
        flops=2 * groups * tokens * near * feat * atts,
        limit=52,
    )
    spread, plain = lax.optimization_barrier((spread, plain))
    plains = [plain[0]] + [lax.ppermute(plain[s], "ep", ahead[s]) for s in range(1, ep_count)]
    fixed = call(
        fixed_kernel,
        [shape_of((slots, atts))] * groups,
        [spread, w_out],
        [VMEM, HBM],
        [VMEM] * groups,
        scratch=[
            pltpu.VMEM((experts * rows, atts), F32),
            pltpu.VMEM(w_out.shape, BF),
            pltpu.SemaphoreType.DMA((near,)),
        ],
        flops=2 * experts * rows * near * feat * atts,
        limit=52,
    )
    spread, fixed = lax.optimization_barrier((spread, fixed))
    fixes = [fixed[0]] + [lax.ppermute(fixed[s], "ep", ahead[s]) for s in range(1, ep_count)]
    (w_out_grad,) = call(
        weight_kernel,
        [shape_of((near * feat, atts))],
        [block, spread.reshape(experts, near, 1, rows, lanes), ctx_all],
        [
            pl.BlockSpec((groups, 1, feat, tokens), lambda j: (0, j, 0, 0)),
            pl.BlockSpec((experts, 1, 1, rows, lanes), lambda j: (0, j, 0, 0, 0)),
            pl.BlockSpec(ctx_all.shape, lambda j: (0, 0)),
        ],
        [pl.BlockSpec((feat, atts), lambda j: (j, 0))],
        grid=(near,),
        flops=2 * groups * tokens * near * feat * atts,
        limit=52,
    )
    resid, ctx_grad = call(
        functools.partial(context_kernel, groups),
        [shape_of((1, feat, tokens)), shape_of((1, atts, tokens))],
        backs + plains + fixes + [out_grad],
        [VMEM] * (3 * groups + 1),
        [VMEM] * 2,
        flops=2 * slots * tokens * (atts + feat),
    )
    return (resid, ctx_grad, w_out_grad) + tuple(grads)


def solution(mesh):
    return jax.shard_map(
        shards,
        mesh=mesh,
        in_specs=(
            P("ep", "tp", None),
            P("ep", "tp", None),
            P("tp"),
            P("ep", "tp", None),
            P("ep", "tp"),
            P("ep", "tp", None),
            P("ep", "tp", None),
            P("ep", "tp", None),
            P("ep", None, None),
            P("ep", None),
            P("ep", None, None),
        ),
        out_specs=(
            P("ep", "tp", None),
            P("ep", "tp", None),
            P("ep", "tp"),
            P("ep", "tp", None),
            P("ep", "tp", None),
            P("ep", "tp", None),
        ),
        check_vma=False,
    )
```

```python
import functools

import jax
import jax.numpy as jnp
from jax import lax
from jax.experimental import pallas as pl
from jax.experimental.pallas import tpu as pltpu
from jax.sharding import PartitionSpec as P

norm_eps = 1e-06
BF = jnp.bfloat16
F32 = jnp.float32
MIB = 1024 * 1024


def mm(left, right):
    return jnp.dot(left, right, preferred_element_type=F32)


def contract_rows(left, right):
    return lax.dot_general(left, right, (((0,), (0,)), ((), ())), preferred_element_type=F32)


def contract_cols(left, right):
    return lax.dot_general(left, right, (((1,), (1,)), ((), ())), preferred_element_type=F32)


def split_two(value):
    high = value.astype(BF).astype(F32)
    rest = jnp.where(jnp.abs(value) < jnp.inf, value - high, 0.0)
    return high, rest


def lane_ids(shape):
    return lax.broadcasted_iota(jnp.int32, shape, len(shape) - 1)


def row_ids(shape):
    return lax.broadcasted_iota(jnp.int32, shape, len(shape) - 2)


def two_lanes(value, shape):
    high, rest = split_two(value)
    lane = lane_ids(shape)
    return jnp.where(lane == 0, high, jnp.where(lane == 1, rest, 0.0))


def call(kernel, outs, operands, in_specs, out_specs, grid=None, scratch=(), flops=0, limit=52):
    size = 0
    for leaf in list(outs) + list(operands):
        count = 1
        for dim in leaf.shape:
            count *= dim
        size += count * leaf.dtype.itemsize
    extra = {} if grid is None else {"grid": grid}
    return pl.pallas_call(
        kernel,
        out_shape=tuple(outs),
        in_specs=in_specs,
        out_specs=tuple(out_specs),
        scratch_shapes=list(scratch),
        compiler_params=pltpu.CompilerParams(vmem_limit_bytes=limit * MIB),
        cost_estimate=pl.CostEstimate(flops=flops, bytes_accessed=size, transcendentals=0),
        **extra,
    )(*operands)


VMEM = pl.BlockSpec(memory_space=pltpu.VMEM)
HBM = pl.BlockSpec(memory_space=pltpu.HBM)


def shape_of(shape, dtype=BF):
    return jax.ShapeDtypeStruct(shape, dtype)


def one_hot(pos, tokens):
    hit = pos.astype(jnp.int32) == lane_ids((pos.shape[0], tokens))
    return jnp.where(hit, 1.0, 0.0).astype(BF)


def pick_kernel(token_ref, count_ref, gate_ref, resid_ref, out_ref, gain_ref, *sends):
    experts, capacity = token_ref.shape[1:]
    feat, tokens = resid_ref.shape[1:]
    lanes = sends[0].shape[1]
    slots = experts * capacity
    ep = lax.axis_index("ep")

    def column(ref):
        rows = []
        for s in range(experts):
            e = lax.rem(ep + s, experts)
            rows.append(jnp.broadcast_to(ref[0, pl.ds(e, 1), :], (capacity, capacity)))
        rows = jnp.concatenate(rows, axis=0)
        shape = (slots, capacity)
        mine = lane_ids(shape) == lax.rem(row_ids(shape), capacity)
        return jnp.sum(jnp.where(mine, rows.astype(F32), 0.0), axis=1, keepdims=True)

    counts = jnp.sum(
        jnp.where(
            lane_ids((slots, experts))
            == lax.rem(ep + row_ids((slots, experts)) // capacity, experts),
            jnp.broadcast_to(count_ref[...], (slots, experts)),
            0,
        ).astype(F32),
        axis=1,
        keepdims=True,
    )
    order = lax.rem(row_ids((slots, 1)), capacity).astype(F32)
    pos = jnp.where(order < counts, column(token_ref), -1.0)
    hot = one_hot(pos, tokens)
    picked = contract_cols(hot, resid_ref[0])
    grads = column(gate_ref) * contract_cols(hot, out_ref[0])
    gained = picked * gain_ref[...]
    for s in range(experts):
        rows = slice(s * capacity, (s + 1) * capacity)
        body = [picked[rows], grads[rows], gained[rows], gained[rows]]
        sends[s][:, :feat] = jnp.concatenate(body, axis=0).astype(BF)
        tail = jnp.concatenate([pos[rows]] * 4, axis=0)
        sends[s][:, feat:] = jnp.broadcast_to(tail, (4 * capacity, lanes - feat)).astype(BF)


def rows_of(blocks, feat):
    blocks = [b[...].astype(F32) for b in blocks]
    capacity = blocks[0].shape[0] // 4
    parts = [
        jnp.concatenate([b[k * capacity : (k + 1) * capacity, :feat] for b in blocks], axis=0)
        for k in range(3)
    ]
    pos = jnp.concatenate([b[:capacity, feat : feat + 1] for b in blocks], axis=0)
    return parts + [pos]


def fetch(sources, buffer, sems, steps):
    tile = buffer.shape[2] // steps
    copies = []
    for i in range(steps):
        part = slice(i * tile, (i + 1) * tile)
        row = []
        for n, source in enumerate(sources):
            row.append(
                pltpu.make_async_copy(
                    source.at[0, :, part], buffer.at[n, :, part], sems.at[n, i]
                )
            )
            row[-1].start()
        copies.append(row)
    return copies


def parts_kernel(features, groups, steps, *refs):
    got = refs[:groups]
    gate_ref, up_ref, down_ref, sums_ref, buffer, sems = refs[groups:]
    copies = fetch((gate_ref, up_ref, down_ref), buffer, sems, steps)
    feat = buffer.shape[1]
    count, _, lanes = sums_ref.shape
    unit = buffer.shape[2] // count
    chunk = count // steps
    tile = unit * chunk
    x, go, gained, _ = rows_of(got, feat)
    gained = gained.astype(BF)
    go = go.astype(BF)
    square = jnp.sum(x * x, axis=1, keepdims=True) / features
    tail = two_lanes(square, (x.shape[0], lanes - 3 * unit)).astype(BF)
    for i in range(steps):
        for n, rows in enumerate((gained, gained, go)):
            copies[i][n].wait()
            part = mm(rows, buffer[n, :, i * tile : (i + 1) * tile]).astype(BF)
            for k in range(chunk):
                u = i * chunk + k
                place = slice(n * unit, (n + 1) * unit)
                sums_ref[u, :, place] = part[:, k * unit : (k + 1) * unit]
        for k in range(chunk):
            u = i * chunk + k
            sums_ref[u, :, 3 * unit :] = tail


def activate(sums, unit):
    square = sums[:, 3 * unit : 3 * unit + 1] + sums[:, 3 * unit + 1 : 3 * unit + 2]
    inv_rms = lax.rsqrt(square + norm_eps)
    pre_gate = jnp.where(inv_rms > 0, sums[:, :unit] * inv_rms, 0.0)
    pre_up = jnp.where(inv_rms > 0, sums[:, unit : 2 * unit] * inv_rms, 0.0)
    hid_grad = sums[:, 2 * unit : 3 * unit]
    sigmoid_gate = 1.0 / (1.0 + jnp.exp(-pre_gate))
    silu_gate = pre_gate * sigmoid_gate
    hidden = (silu_gate * pre_up).astype(BF)
    d_gate = (hid_grad * pre_up * sigmoid_gate * (1.0 + pre_gate * (1.0 - sigmoid_gate))).astype(BF)
    d_up = (hid_grad * silu_gate).astype(BF)
    dots = jnp.sum(
        d_gate.astype(F32) * pre_gate + d_up.astype(F32) * pre_up, axis=1, keepdims=True
    )
    tail = two_lanes(dots, (sums.shape[0], sums.shape[1] - 3 * unit)).astype(BF)
    return inv_rms, jnp.concatenate([hidden, d_gate, d_up, tail], axis=1)


def act_kernel(unit, sums_ref, inv_ref, acts_ref):
    total = sums_ref[0].astype(F32)
    for k in range(1, sums_ref.shape[0]):
        total = total + sums_ref[k].astype(F32)
    inv_rms, acts = activate(total, unit)
    inv_ref[...] = jnp.broadcast_to(inv_rms, inv_ref.shape)
    for k in range(acts_ref.shape[0]):
        acts_ref[k] = acts


def delta_kernel(features, unit, groups, steps, *refs):
    got = refs[:groups]
    acts_ref, gain_ref, inv_ref, gate_ref, up_ref = refs[groups : groups + 5]
    hidden_ref, dgate_ref, dup_ref, slot_ref, go_ref, delta_ref = refs[groups + 5 : groups + 11]
    backs = refs[groups + 11 : 2 * groups + 11]
    buffer, sems = refs[2 * groups + 11 :]
    copies = fetch((gate_ref, up_ref), buffer, sems, steps)
    feat = buffer.shape[1]
    count = acts_ref.shape[0]
    chunk = count // steps
    tile = unit * chunk
    x, go, _, pos = rows_of(got, feat)
    inv_rms = inv_ref[:, :1]
    normed = x * inv_rms
    slot_ref[...] = (normed * gain_ref[:1]).astype(BF)
    go_ref[...] = go.astype(BF)
    dots = acts_ref[0, :, 3 * unit : 3 * unit + 128].astype(F32)
    for u in range(1, count):
        dots = dots + acts_ref[u, :, 3 * unit : 3 * unit + 128].astype(F32)
    dots = (dots[:, :1] + dots[:, 1:2]) / features
    total = jnp.zeros((x.shape[0], feat), F32)
    for i in range(steps):
        part = slice(i * tile, (i + 1) * tile)
        for n, ref in enumerate((hidden_ref, dgate_ref, dup_ref)):
            place = slice(n * unit, (n + 1) * unit)
            value = jnp.concatenate(
                [acts_ref[u, :, place] for u in range(i * chunk, (i + 1) * chunk)],
                axis=1,
            )
            ref[:, part] = value
            if n > 0:
                copies[i][n - 1].wait()
                total = total + contract_cols(value, buffer[n - 1, :, part])
    change = inv_rms * (total * gain_ref[:1] - normed * dots)
    tail = jnp.broadcast_to(pos, (pos.shape[0], delta_ref.shape[1] - feat))
    delta_ref[:, :feat] = change.astype(BF)
    delta_ref[:, feat:] = tail.astype(BF)
    capacity = backs[0].shape[0]
    for s in range(groups):
        rows = slice(s * capacity, (s + 1) * capacity)
        backs[s][:, :feat] = change[rows]
        backs[s][:, feat:] = tail[rows]


def grads_kernel(
    steps, slot_ref, go_ref, hidden_ref, dgate_ref, dup_ref,
    gate_out, up_out, down_out, buffer, sems,
):
    tile = buffer.shape[2] // steps
    work = ((slot_ref, dgate_ref, gate_out), (slot_ref, dup_ref, up_out), (go_ref, hidden_ref, down_out))
    copies = []
    for i in range(steps):
        part = slice(i * tile, (i + 1) * tile)
        for n, (rows, units, out) in enumerate(work):
            buffer[n, :, part] = contract_rows(rows[...], units[:, part]).astype(BF)
            copies.append(
                pltpu.make_async_copy(buffer.at[n, :, part], out.at[0, :, part], sems.at[n, i])
            )
            copies[-1].start()
    for copy in copies:
        copy.wait()


def back_rows(backs, feat):
    rows = jnp.concatenate([b[...] for b in backs], axis=0)
    return rows[:, :feat].astype(BF), rows[:, feat : feat + 1]


def plain_kernel(steps, block_ref, w_ref, *refs):
    outs, (acc_ref, block, weights, sems) = refs[:-4], refs[-4:]
    groups, near, feat, tokens = block.shape
    cores = near // steps
    ep = lax.axis_index("ep")
    copies = []
    for q in range(steps):
        part = slice(q * cores, (q + 1) * cores)
        rows = slice(q * cores * feat, (q + 1) * cores * feat)
        copies.append(
            (
                pltpu.make_async_copy(block_ref.at[:, part], block.at[:, part], sems.at[0, q]),
                pltpu.make_async_copy(w_ref.at[rows, :], weights.at[rows, :], sems.at[1, q]),
            )
        )
        for copy in copies[-1]:
            copy.start()
    for q in range(steps):
        for copy in copies[q]:
            copy.wait()
        columns = []
        for shift in range(groups):
            g = lax.rem(ep + shift, groups)
            columns.append(jnp.concatenate([block[g, q * cores + c] for c in range(cores)], axis=0))
        rows = slice(q * cores * feat, (q + 1) * cores * feat)
        part = contract_rows(jnp.concatenate(columns, axis=1), weights[rows, :])
        acc_ref[...] = part if q == 0 else acc_ref[...] + part
    for shift in range(groups):
        outs[shift][...] = acc_ref[shift * tokens : (shift + 1) * tokens, :].astype(BF)


def fixed_kernel(delta_ref, w_ref, *refs):
    outs, (acc_ref, buffer, sems) = refs[:-3], refs[-3:]
    experts, quarters, cores, rows, _ = delta_ref.shape
    groups = len(outs)
    capacity = rows // groups
    feat = w_ref.shape[0] // (quarters * cores)
    ep = lax.axis_index("ep")
    copies = []
    for j in range(quarters * cores):
        part = slice(j * feat, (j + 1) * feat)
        copies.append(pltpu.make_async_copy(w_ref.at[part, :], buffer.at[part, :], sems.at[j]))
        copies[-1].start()
    for j in range(quarters * cores):
        delta = [delta_ref[e, j // cores, j % cores] for e in range(experts)]
        delta = jnp.concatenate(delta, axis=0)[:, :feat]
        copies[j].wait()
        part = mm(delta, buffer[j * feat : (j + 1) * feat, :])
        acc_ref[...] = part if j == 0 else acc_ref[...] + part
    for shift in range(groups):
        pieces = []
        for s in range(experts):
            e = lax.rem(ep + shift + s, experts)
            start = pl.multiple_of(e * rows + s * capacity, 8)
            pieces.append(acc_ref[pl.ds(start, capacity), :])
        outs[shift][...] = jnp.concatenate(pieces, axis=0).astype(BF)


def weight_kernel(block_ref, delta_ref, ctx_ref, out_ref, block, result, sems):
    groups, near, feat, tokens = block.shape
    experts, steps, cores, rows, _ = delta_ref.shape
    capacity = rows // groups
    ep = lax.axis_index("ep")
    arrive, leave = [], []
    for q in range(steps):
        part = slice(q * cores, (q + 1) * cores)
        arrive.append(pltpu.make_async_copy(block_ref.at[:, part], block.at[:, part], sems.at[0, q]))
        arrive[-1].start()
    columns = experts * rows
    row = row_ids((columns, 1))
    group_of = lax.rem(row // rows - lax.rem(row // capacity, groups) + groups, groups)
    order = [lax.rem(ep - shift + groups, groups) for shift in range(groups)]
    packed = jnp.concatenate([delta_ref[e, 0, 0] for e in range(experts)], axis=0)
    pos = packed[:, feat : feat + 1].astype(F32)
    hot = jnp.concatenate(
        [one_hot(jnp.where(group_of == g, pos, -1.0), tokens) for g in order], axis=1
    )
    for q in range(steps):
        arrive[q].wait()
        blocks = []
        for c in range(cores):
            delta = [delta_ref[e, q, c] for e in range(experts)]
            delta = jnp.concatenate(delta, axis=0)[:, :feat]
            plain = jnp.concatenate([block[g, q * cores + c] for g in order], axis=1)
            blocks.append((plain.astype(F32) + contract_rows(delta, hot)).astype(BF))
        part = slice(q * cores * feat, (q + 1) * cores * feat)
        result[part, :] = mm(jnp.concatenate(blocks, axis=0), ctx_ref[...]).astype(BF)
        leave.append(pltpu.make_async_copy(result.at[part, :], out_ref.at[part, :], sems.at[1, q]))
        leave[-1].start()
    for copy in leave:
        copy.wait()


def context_kernel(groups, *refs):
    grad_ref, resid_ref, out_ref = refs[-3:]
    tokens = out_ref.shape[2]
    backs, plains, fixes = refs[:groups], refs[groups : 2 * groups], refs[2 * groups : -3]
    change, pos = back_rows(backs, grad_ref.shape[1])
    hot = one_hot(pos, tokens)
    resid_ref[0] = (grad_ref[0].astype(F32) + contract_rows(change, hot)).astype(BF)
    total = plains[0][...].astype(F32)
    for ref in plains[1:]:
        total = total + ref[...].astype(F32)
    for ref in fixes:
        total = total + contract_rows(hot, ref[...])
    out_ref[0] = total.T.astype(BF)


def shards(
    residual,
    out_grad,
    norm_gain,
    context,
    w_out,
    w_gate,
    w_up,
    w_down,
    slot_token,
    slot_count,
    slot_gate,
):
    tp_count = lax.axis_size("tp")
    ep_count = lax.axis_size("ep")
    near = tp_count // ep_count
    feat, tokens = residual.shape[1:]
    features = feat * tp_count
    experts, capacity = slot_token.shape[1:]
    groups = ep_count
    slots = experts * capacity
    rows = groups * capacity
    hidden_units = w_gate.shape[2]
    unit = hidden_units // tp_count
    atts = w_out.shape[1]
    lanes = -(-(feat + 1) // 128) * 128
    gain_row = norm_gain[None, :]
    ahead = [[(i, (i + s) % ep_count) for i in range(ep_count)] for s in range(ep_count)]
    behind = [[(i, (i - s) % ep_count) for i in range(ep_count)] for s in range(ep_count)]

    sends = call(
        pick_kernel,
        [shape_of((4 * capacity, lanes))] * experts,
        [slot_token, slot_count, slot_gate, residual, out_grad, norm_gain[None, :]],
        [VMEM] * 6,
        [VMEM] * experts,
        flops=4 * slots * tokens * feat,
        limit=56,
    )
    got = [sends[0]] + [lax.ppermute(sends[s], "ep", ahead[s]) for s in range(1, ep_count)]

    route = []
    for a in range(tp_count):
        for b in range(ep_count):
            route.append((a * ep_count + b, (b * near + a % near) * ep_count + a // near))
    moved = lax.ppermute(out_grad[0], ("tp", "ep"), route)

    steps = 4
    tile = hidden_units // steps
    wide = 3 * unit + 128
    if unit % 128 == 0:
        (sums,) = call(
            functools.partial(parts_kernel, features, groups, steps),
            [shape_of((tp_count, rows, wide))],
            got + [w_gate, w_up, w_down],
            [VMEM] * groups + [HBM] * 3,
            [VMEM],
            scratch=[
                pltpu.VMEM((3, feat, hidden_units), BF),
                pltpu.SemaphoreType.DMA((3, steps)),
            ],
            flops=6 * rows * feat * hidden_units,
        )
    else:
        x, go, gained, _ = rows_of(got, feat)
        gained = gained.astype(BF)
        square = jnp.sum(x * x, axis=1, keepdims=True) / features
        parts = [mm(gained, w_gate[0]), mm(gained, w_up[0]), mm(go.astype(BF), w_down[0])]
        parts = [p.astype(BF).reshape(rows, tp_count, unit).transpose(1, 0, 2) for p in parts]
        tail = two_lanes(square, (rows, 128)).astype(BF)
        tail = jnp.broadcast_to(tail[None], (tp_count, rows, 128))
        sums = jnp.concatenate(parts + [tail], axis=2)
    sums, moved = lax.optimization_barrier((sums, moved))
    block = lax.all_gather(moved, "tp", axis=0).reshape(groups, near, feat, tokens)
    sums = lax.all_to_all(sums, "tp", split_axis=0, concat_axis=0, tiled=True)
    if unit % 128 == 0:
        inv_rms, acts = call(
            functools.partial(act_kernel, unit),
            [shape_of((rows, 128), F32), shape_of((tp_count, rows, wide))],
            [sums],
            [VMEM],
            [VMEM, VMEM],
        )
    else:
        inv_rms, acts = activate(jnp.sum(sums.astype(F32), axis=0), unit)
        inv_rms = jnp.broadcast_to(inv_rms, (rows, 128))
        acts = jnp.broadcast_to(acts[None], (tp_count,) + acts.shape)
    acts, ctx_own = lax.optimization_barrier((acts, context[0]))
    acts = lax.all_to_all(acts, "tp", split_axis=0, concat_axis=0, tiled=True)

    ctx_own = ctx_own.T
    ctx_parts = [ctx_own] + [lax.ppermute(ctx_own, "ep", ahead[s]) for s in range(1, ep_count)]
    ctx_all = jnp.concatenate(ctx_parts, axis=0)
    acts, ctx_all = lax.optimization_barrier((acts, ctx_all))
    if unit % 128 == 0:
        made = call(
            functools.partial(delta_kernel, features, unit, groups, steps),
            [shape_of((rows, hidden_units))] * 3
            + [shape_of((rows, feat))] * 2
            + [shape_of((rows, lanes))]
            + [shape_of((capacity, lanes), F32)] * groups,
            got + [acts, gain_row, inv_rms, w_gate, w_up],
            [VMEM] * (groups + 3) + [HBM] * 2,
            [VMEM] * (6 + groups),
            scratch=[
                pltpu.VMEM((2, feat, hidden_units), BF),
                pltpu.SemaphoreType.DMA((2, steps)),
            ],
            flops=4 * rows * feat * hidden_units,
        )
        hidden, d_gate, d_up, slot_in, rows_go, delta = made[:6]
        backs = list(made[6:])
    else:
        x, go, _, pos = rows_of(got, feat)
        rows_go = go.astype(BF)
        hidden, d_gate, d_up = [
            acts[:, :, n * unit : (n + 1) * unit].transpose(1, 0, 2).reshape(rows, hidden_units)
            for n in range(3)
        ]
        dots = jnp.sum(acts[:, :, 3 * unit : 3 * unit + 2].astype(F32), axis=(0, 2))[:, None]
        normed = x * inv_rms[:, :1]
        slot_in = (normed * norm_gain[None, :]).astype(BF)
        slot_back = contract_cols(d_gate, w_gate[0]) + contract_cols(d_up, w_up[0])
        change = inv_rms[:, :1] * (slot_back * norm_gain[None, :] - normed * (dots / features))
        packed = jnp.concatenate([change, jnp.broadcast_to(pos, (rows, lanes - feat))], axis=1)
        delta = packed.astype(BF)
        backs = [packed[s * capacity : (s + 1) * capacity] for s in range(groups)]

    spread = lax.ppermute(delta, ("tp", "ep"), route)
    backs = [backs[0]] + [lax.ppermute(backs[s], "ep", behind[s]) for s in range(1, ep_count)]
    grads = call(
        functools.partial(grads_kernel, steps),
        [shape_of((1, feat, hidden_units))] * 3,
        [slot_in, rows_go, hidden, d_gate, d_up],
        [VMEM] * 5,
        [HBM] * 3,
        scratch=[
            pltpu.VMEM((3, feat, hidden_units), BF),
            pltpu.SemaphoreType.DMA((3, steps)),
        ],
        flops=6 * rows * feat * hidden_units,
    )
    spread, grads = lax.optimization_barrier((spread, grads))
    spread = jnp.broadcast_to(spread[None], (tp_count, rows, lanes))
    spread = lax.all_to_all(spread, "tp", split_axis=0, concat_axis=0, tiled=True)
    spread = spread.reshape(experts, near // 2, 2, rows, lanes)

    quarters = near // 2
    plain = call(
        functools.partial(plain_kernel, quarters),
        [shape_of((tokens, atts))] * groups,
        [block, w_out],
        [HBM] * 2,
        [VMEM] * groups,
        scratch=[
            pltpu.VMEM((groups * tokens, atts), F32),
            pltpu.VMEM(block.shape, BF),
            pltpu.VMEM(w_out.shape, BF),
            pltpu.SemaphoreType.DMA((2, quarters)),
        ],
        flops=2 * groups * tokens * near * feat * atts,
    )
    spread, plain = lax.optimization_barrier((spread, plain))
    plains = [plain[0]] + [lax.ppermute(plain[s], "ep", ahead[s]) for s in range(1, ep_count)]
    fixed = call(
        fixed_kernel,
        [shape_of((slots, atts))] * groups,
        [spread, w_out],
        [VMEM, HBM],
        [VMEM] * groups,
        scratch=[
            pltpu.VMEM((experts * rows, atts), F32),
            pltpu.VMEM(w_out.shape, BF),
            pltpu.SemaphoreType.DMA((near,)),
        ],
        flops=2 * experts * rows * near * feat * atts,
        limit=52,
    )
    spread, fixed = lax.optimization_barrier((spread, fixed))
    fixes = [fixed[0]] + [lax.ppermute(fixed[s], "ep", ahead[s]) for s in range(1, ep_count)]
    (w_out_grad,) = call(
        weight_kernel,
        [shape_of((near * feat, atts))],
        [block, spread, ctx_all],
        [HBM, VMEM, VMEM],
        [HBM],
        scratch=[
            pltpu.VMEM(block.shape, BF),
            pltpu.VMEM((near * feat, atts), BF),
            pltpu.SemaphoreType.DMA((2, quarters)),
        ],
        flops=2 * groups * tokens * near * feat * atts,
    )
    resid, ctx_grad = call(
        functools.partial(context_kernel, groups),
        [shape_of((1, feat, tokens)), shape_of((1, atts, tokens))],
        backs + plains + fixes + [out_grad],
        [VMEM] * (3 * groups + 1),
        [VMEM] * 2,
        flops=2 * slots * tokens * (atts + feat),
    )
    return (resid, ctx_grad, w_out_grad) + tuple(grads)


def solution(mesh):
    return jax.shard_map(
        shards,
        mesh=mesh,
        in_specs=(
            P("ep", "tp", None),
            P("ep", "tp", None),
            P("tp"),
            P("ep", "tp", None),
            P("ep", "tp"),
            P("ep", "tp", None),
            P("ep", "tp", None),
            P("ep", "tp", None),
            P("ep", None, None),
            P("ep", None),
            P("ep", None, None),
        ),
        out_specs=(
            P("ep", "tp", None),
            P("ep", "tp", None),
            P("ep", "tp"),
            P("ep", "tp", None),
            P("ep", "tp", None),
            P("ep", "tp", None),
        ),
        check_vma=False,
    )
```
